32 devices in a mesh: seq: 8 (over z, core), tp: 4 (over y, x).
Axes of the slice: x: 2, y: 2, z: 4, core: 2. Of those that a mesh axis runs over, the one named last changes fastest.
Arguments:
- inputs: bfloat16 [24576, 1024], P('seq'), may hold values from -6 to 6
- w_in: bfloat16 [3, 1024, 1024], P(None, None, 'tp'), may hold values from -0.1875 to 0.1875
- conv_w: bfloat16 [3, 1024], P(None, 'tp'), may hold values from -3.5 to 3.5
- w_out: bfloat16 [1024, 1024], P('tp'), may hold values from -0.1875 to 0.1875
- norm_one: bfloat16 [1024], replicated, may hold values from 0.5 to 1.5
- norm_two: bfloat16 [1024], replicated, may hold values from 0.5 to 1.5
- w_gate: bfloat16 [1024, 4608], P(None, 'tp'), may hold values from -0.1875 to 0.1875
- w_up: bfloat16 [1024, 4608], P(None, 'tp'), may hold values from -0.1875 to 0.1875
- w_down: bfloat16 [4608, 1024], P('tp'), may hold values from -0.09375 to 0.09375
- lengths: int32 [6], replicated, may hold values from 2048 to 4096, as said below
- cotangent: bfloat16 [24576, 1024], P('seq'), may hold values from -6 to 6
Outputs:
- output: bfloat16 [24576, 1024], P('seq')
- grad_inputs: float32 [24576, 1024], P('seq')
- grad_w_in: float32 [3, 1024, 1024], P(None, None, 'tp')
- grad_conv: float32 [3, 1024], P(None, 'tp')
- grad_w_out: float32 [1024, 1024], P('tp')
- grad_norm_one: float32 [1024], replicated
- grad_norm_two: float32 [1024], replicated
- grad_w_gate: float32 [1024, 4608], P(None, 'tp')
- grad_w_up: float32 [1024, 4608], P(None, 'tp')
- grad_w_down: float32 [4608, 1024], P('tp')
The draws below stay inside these ranges and needn't reach their ends.
Inputs may be any that keep to these rules, and one draw needn't show every extreme that they name: `lengths`: one sequence, drawn from the seed, has length 4096; the others at least half of it.
All inputs are finite; a program needn't handle non-finite values.
Results may differ from the reference program's by a relative error of at most 0.011.
Values may be sent and summed in bfloat16 or wider, within the bound.
No kernel may reach another device: no remote copies, remote signals or barrier semaphores. Data moves between devices by JAX's collectives and lax.ppermute only.
A program may use at most 256 MiB of HBM per device.

```python
import jax
import jax.numpy as jnp
from jax import lax

D = 1024
FF = 4608
SEQS = 6
TOKENS = 24576
SLOT = 4096


def draw_lengths(key, part):
    key = jax.random.fold_in(key, 7)
    base = jax.random.randint(jax.random.fold_in(key, 1), (SEQS,), SLOT // 2, SLOT + 1)
    picked = jax.random.randint(jax.random.fold_in(key, 2), (), 0, SEQS)
    return jnp.where(jnp.arange(SEQS) == picked, SLOT, base).astype(jnp.int32)


def levels(key, dims, cuts, smallest, high):
    def one(position, shards_of):
        steps = jax.random.uniform(jax.random.fold_in(jax.random.fold_in(key, 6), position), (shards_of,), jnp.float32, smallest / len(cuts), high / len(cuts))
        return jnp.repeat(jnp.exp(steps), dims[position] // shards_of).reshape((-1,) + (1,) * (len(dims) - position - 1))

    level = one(*cuts[0])
    for cut in cuts[1:]:
        level = level * one(*cut)
    return level


def gaussian(rng, extent, width, bound, split=(), kind=jnp.bfloat16):
    values = jax.random.normal(rng, extent, jnp.float32) * width
    if len(split) > 0:
        values = levels(rng, extent, split, -0.22, 0.18) * values
    return jnp.clip(values, min=-bound, max=bound).astype(kind)


def setup_inputs(seed: int = 0) -> dict:
    key_list = jax.random.split(jax.random.key(seed), 12)
    return {
        "inputs": gaussian(key_list[0], (TOKENS, D), 1.0, 6.0, ((0, 8),)),
        "w_in": gaussian(key_list[1], (3, D, D), D ** -0.5, 0.1875, ((2, 4),)),
        "conv_w": gaussian(key_list[2], (3, D), 3 ** -0.5, 3.5, ((1, 4),)),
        "w_out": gaussian(key_list[3], (D, D), D ** -0.5, 0.1875, ((0, 4),)),
        "norm_one": jnp.clip(1.0 + 0.1 * jax.random.normal(key_list[4], (D,), jnp.float32), 0.5, 1.5).astype(jnp.bfloat16),
        "norm_two": jnp.clip(1.0 + 0.1 * jax.random.normal(key_list[5], (D,), jnp.float32), 0.5, 1.5).astype(jnp.bfloat16),
        "w_gate": gaussian(key_list[6], (D, FF), D ** -0.5, 0.1875, ((1, 4),)),
        "w_up": gaussian(key_list[7], (D, FF), D ** -0.5, 0.1875, ((1, 4),)),
        "w_down": gaussian(key_list[8], (FF, D), FF ** -0.5, 0.09375, ((0, 4),)),
        "lengths": draw_lengths(jax.random.fold_in(key_list[11], 71), 0),
        "cotangent": gaussian(key_list[10], (TOKENS, D), 1.0, 6.0, ((0, 8),)),
    }


@jax.custom_vjp
def low(v):
    return lax.optimization_barrier(v.astype(jnp.bfloat16)).astype(jnp.float32)

@jax.custom_vjp
def low_back(v):
    return v

def low_keep(v):
    return (low(v), None)

def low_pass(kept, grad):
    return (grad,)

def back_keep(v):
    return (v, None)

def back_low(kept, grad):
    return (low(grad),)
low.defvjp(low_keep, low_pass)
low_back.defvjp(back_keep, back_low)

def mult(left, right):
    return jnp.dot(left, right, precision=lax.Precision.HIGHEST, preferred_element_type=jnp.float32)

def rms_norm(values, gain):
    scale = lax.rsqrt(lax.optimization_barrier(jnp.mean(values * values, axis=1, keepdims=True)) + 1e-05)
    return values * scale * gain[None, :]

def sequence_layer(xfull, params):
    w_in, conv_w, w_out, norm_one, norm_two, w_gate, w_up, w_down = params
    hidden_one = low(rms_norm(xfull, norm_one))
    proj_b = low_back(mult(hidden_one, w_in[0]))
    proj_c = low_back(mult(hidden_one, w_in[1]))
    proj_x = low_back(mult(hidden_one, w_in[2]))
    mixed_in = low(proj_b * proj_x)
    padded = jnp.concatenate([jnp.zeros((2, mixed_in.shape[1]), mixed_in.dtype), mixed_in], axis=0)
    conved = conv_w[2][None, :] * mixed_in + conv_w[1][None, :] * padded[1:-1] + conv_w[0][None, :] * padded[:-2]
    gated = low(proj_c * conved)
    resid = xfull + low_back(mult(gated, w_out))
    hidden_two = low(rms_norm(resid, norm_two))
    gate_pre = low_back(mult(hidden_two, w_gate))
    up_pre = low_back(mult(hidden_two, w_up))
    activ = low(jax.nn.silu(gate_pre) * up_pre)
    return resid + low_back(mult(activ, w_down))

def reference(inputs, w_in, conv_w, w_out, norm_one, norm_two, w_gate, w_up, w_down, lengths, cotangent):
    floats = jnp.float32
    xs = inputs.astype(floats).reshape(SEQS, SLOT, D)
    params = (w_in.astype(floats), conv_w.astype(floats), w_out.astype(floats), norm_one.astype(floats), norm_two.astype(floats), w_gate.astype(floats), w_up.astype(floats), w_down.astype(floats))

    def whole(values, weights):

        def one_sequence(single):
            return sequence_layer(single, weights)
        return lax.map(jax.checkpoint(one_sequence), values)
    result, pullback = jax.vjp(whole, xs, params)
    real = (jnp.arange(SLOT, dtype=jnp.int32)[None, :] < lengths.astype(jnp.int32)[:, None]).astype(floats)
    masked = cotangent.astype(floats).reshape(SEQS, SLOT, D) * real[:, :, None]
    grad_xs, grads = pullback(masked)
    return (result.reshape(TOKENS, D).astype(jnp.bfloat16), grad_xs.reshape(TOKENS, D), grads[0], grads[1], grads[2], grads[3], grads[4], grads[5], grads[6], grads[7])
```

```python
import functools

import jax
import jax.numpy as jnp
from jax import lax
from jax.experimental import pallas as pl
from jax.experimental.pallas import tpu as pltpu
from jax.sharding import PartitionSpec as P

SEQS = 6
F32 = jnp.float32
BF16 = jnp.bfloat16
VMEM_LIMIT = 56 * 2**20


def params():
    return pltpu.CompilerParams(vmem_limit_bytes=VMEM_LIMIT)


def cost(flops, moved):
    return pl.CostEstimate(flops=int(flops), bytes_accessed=int(moved), transcendentals=0)


def nbytes(*arrays):
    return sum(a.size * a.dtype.itemsize for a in arrays)


def shape(dims, dtype):
    return jax.ShapeDtypeStruct(dims, dtype)


def dot(left, right):
    return jnp.dot(left, right, preferred_element_type=F32)


def dot_nt(left, right):
    return lax.dot_general(left, right, (((1,), (1,)), ((), ())), preferred_element_type=F32)


def dot_tn(left, right):
    return lax.dot_general(left, right, (((0,), (0,)), ((), ())), preferred_element_type=F32)


def rms_scale(values):
    return lax.rsqrt(jnp.mean(values * values, axis=1, keepdims=True) + 1e-05)


def resident(array):
    zeros = (0,) * array.ndim
    return pl.BlockSpec(array.shape, lambda i, *_: zeros, pipeline_mode=pl.Buffered(1))


def mixer_forward_body(slot, base, x, halo, gain_one, gain_two, taps, w_b, w_c, w_x, w_out,
                       h1, p_b, p_c, p_x, conv, gated, resid, h2, carry):
    step = pl.program_id(0)
    rows = x.shape[0]

    def hidden(values):
        wide = values.astype(F32)
        return wide, ((wide * rms_scale(wide)) * gain_one[...]).astype(BF16)

    @pl.when(step == 0)
    def _():
        _, before = hidden(halo[...])
        mixed = (dot(before, w_b[...]) * dot(before, w_x[...])).astype(BF16).astype(F32)
        carry[...] = mixed[8:16]

    wide, low = hidden(x[...])
    h1[...] = low
    b = dot(low, w_b[...])
    xx = dot(low, w_x[...])
    c = dot(low, w_c[...])
    p_b[...] = b.astype(BF16)
    p_x[...] = xx.astype(BF16)
    p_c[...] = c.astype(BF16)
    mixed = (b * xx).astype(BF16).astype(F32)
    fresh = lax.rem(base[0] + step * rows, slot) == 0
    last = jnp.where(fresh, 0.0, carry[...])
    row = lax.broadcasted_iota(jnp.int32, mixed.shape, 0)
    one = jnp.where(row == 0, last[7:8], pltpu.roll(mixed, 1, 0))
    two = jnp.where(row == 0, last[6:7], jnp.where(row == 1, last[7:8], pltpu.roll(mixed, 2, 0)))
    carry[...] = mixed[rows - 8:]
    conved = taps[2:3] * mixed + taps[1:2] * one + taps[0:1] * two
    conv[...] = conved.astype(BF16)
    gate = (c * conved).astype(BF16)
    gated[...] = gate
    res = wide + dot(gate, w_out[...])
    resid[...] = res
    h2[...] = ((res * rms_scale(res)) * gain_two[...]).astype(BF16)


def mixer_forward(slot, base, x, halo, gain_one, gain_two, taps, w_b, w_c, w_x, w_out, tile=256):
    rows, width = x.shape
    chans = w_b.shape[1]
    row = lambda n: pl.BlockSpec((tile, n), lambda i, *_: (i, 0))
    outs = [shape((rows, width), BF16)] + [shape((rows, chans), BF16)] * 5 + [
        shape((rows, width), F32), shape((rows, width), BF16)]
    return pl.pallas_call(
        functools.partial(mixer_forward_body, slot),
        grid_spec=pltpu.PrefetchScalarGridSpec(
            num_scalar_prefetch=1,
            grid=(rows // tile,),
            in_specs=[row(width)] + [resident(a) for a in (halo, gain_one, gain_two, taps, w_b, w_c, w_x, w_out)],
            out_specs=[row(s.shape[1]) for s in outs],
            scratch_shapes=[pltpu.VMEM((8, chans), F32)],
        ),
        out_shape=outs,
        compiler_params=params(),
        cost_estimate=cost(8 * rows * width * chans, nbytes(x, w_b, w_c, w_x, w_out, *outs)),
        name="mixer_forward",
    )(base, x, halo, gain_one, gain_two, taps, w_b, w_c, w_x, w_out)


def ffn_body(h2, grad, w_gu, w_down, out, back, activ, grads):
    units = w_down.shape[0]
    both = dot(h2[...], w_gu[...])
    d_activ = dot_nt(grad[...], w_down[...])
    gate = both[:, :units]
    up = both[:, units:]
    sig = 1.0 / (1.0 + jnp.exp(-gate))
    silu = gate * sig
    act = (silu * up).astype(BF16)
    g_gate = (d_activ * up * sig * (1.0 + gate * (1.0 - sig))).astype(BF16)
    g_up = (d_activ * silu).astype(BF16)
    activ[...] = act
    pair = jnp.concatenate([g_gate, g_up], axis=1)
    grads[...] = pair
    out[...] = dot(act, w_down[...]).astype(BF16)
    back[...] = dot_nt(pair, w_gu[...]).astype(BF16)


def ffn(h2, grad, w_gu, w_down, tile=256):
    rows, width = h2.shape
    units = w_down.shape[0]
    row = lambda n: pl.BlockSpec((tile, n), lambda i: (i, 0))
    outs = [shape((rows, width), BF16)] * 2 + [shape((rows, units), BF16), shape((rows, 2 * units), BF16)]
    return pl.pallas_call(
        ffn_body,
        grid=(rows // tile,),
        in_specs=[row(width), row(width), resident(w_gu), resident(w_down)],
        out_specs=[row(s.shape[1]) for s in outs],
        out_shape=outs,
        compiler_params=params(),
        cost_estimate=cost(12 * rows * width * units, nbytes(h2, grad, w_gu, w_down, *outs)),
        name="ffn",
    )(h2, grad, w_gu, w_down)


def weight_grad_body(left, right, out):
    out[...] = dot_tn(left[...], right[...])


def weight_grad(left, right):
    rows, high = left.shape
    wide = right.shape[1]
    tile = next(t for t in (768, 640, 512, 384, 256, 128) if wide % t == 0)
    return pl.pallas_call(
        weight_grad_body,
        grid=(wide // tile,),
        in_specs=[resident(left), pl.BlockSpec((rows, tile), lambda i: (0, i))],
        out_specs=pl.BlockSpec((high, tile), lambda i: (0, i)),
        out_shape=shape((high, wide), F32),
        compiler_params=params(),
        cost_estimate=cost(2 * rows * high * wide, nbytes(left, right) + 4 * high * wide),
        name="weight_grad",
    )(left, right)


def mixer_backward_body(slot, own, base, grl, x, p_b, p_c, p_x, conv, next_grl, next_c, gain_one, taps,
                        w_b, w_c, w_x, w_out, g_in, g_proj, g_conv, g_norm, carry):
    step = pl.program_id(0)
    steps = pl.num_programs(0)
    rows = x.shape[0]

    @pl.when(step == 0)
    def _():
        after = dot_nt(next_grl[...], w_out[...]) * next_c[...].astype(F32)
        carry[...] = after[0:8]
        g_conv[...] = jnp.zeros_like(g_conv)
        g_norm[...] = jnp.zeros_like(g_norm)

    d_gated = dot_nt(grl[...], w_out[...])
    d_conv = d_gated * p_c[...].astype(F32)
    g_c = (d_gated * conv[...].astype(F32)).astype(BF16)
    fresh = lax.rem(base[0] + (steps - step) * rows, slot) == 0
    first = jnp.where(fresh, 0.0, carry[...])
    row = lax.broadcasted_iota(jnp.int32, d_conv.shape, 0)
    one = jnp.where(row == rows - 1, first[0:1], pltpu.roll(d_conv, rows - 1, 0))
    two = jnp.where(row == rows - 2, first[0:1],
                    jnp.where(row == rows - 1, first[1:2], pltpu.roll(d_conv, rows - 2, 0)))
    carry[...] = d_conv[0:8]
    b = p_b[...].astype(F32)
    xx = p_x[...].astype(F32)
    mixed = (b[:, :own] * xx[:, :own]).astype(BF16).astype(F32)
    g_conv[0:1] += jnp.sum(two[:, :own] * mixed, axis=0, keepdims=True)
    g_conv[1:2] += jnp.sum(one[:, :own] * mixed, axis=0, keepdims=True)
    g_conv[2:3] += jnp.sum(d_conv[:, :own] * mixed, axis=0, keepdims=True)
    d_mixed = taps[2:3] * d_conv + taps[1:2] * one + taps[0:1] * two
    g_b = (d_mixed * xx).astype(BF16)
    g_x = (d_mixed * b).astype(BF16)
    g_proj[...] = jnp.concatenate([g_b[:, :own], g_c[:, :own], g_x[:, :own]], axis=1)
    d_hidden = dot_nt(g_b, w_b[...]) + dot_nt(g_c, w_c[...]) + dot_nt(g_x, w_x[...])
    wide = x[...].astype(F32)
    scale = rms_scale(wide)
    normed = wide * scale
    g_norm[0:1] += jnp.sum(d_hidden * normed, axis=0, keepdims=True)
    d_normed = d_hidden * gain_one[...]
    g_in[...] = grl[...].astype(F32) + scale * (
        d_normed - normed * jnp.mean(d_normed * normed, axis=1, keepdims=True))


def mixer_backward(slot, own, base, grl, x, p_b, p_c, p_x, conv, next_grl, next_c, gain_one, taps,
                   w_b, w_c, w_x, w_out, tile=256):
    rows, width = x.shape
    chans = w_b.shape[1]
    steps = rows // tile
    row = lambda n: pl.BlockSpec((tile, n), lambda i, *_: (steps - 1 - i, 0))
    whole = lambda dims: pl.BlockSpec(dims, lambda i, *_: (0, 0))
    outs = [shape((rows, width), F32), shape((rows, 3 * own), BF16), shape((8, own), F32), shape((8, width), F32)]
    return pl.pallas_call(
        functools.partial(mixer_backward_body, slot, own),
        grid_spec=pltpu.PrefetchScalarGridSpec(
            num_scalar_prefetch=1,
            grid=(steps,),
            in_specs=[row(width), row(width)] + [row(chans)] * 4
            + [resident(a) for a in (next_grl, next_c, gain_one, taps, w_b, w_c, w_x, w_out)],
            out_specs=[row(width), row(3 * own), whole((8, own)), whole((8, width))],
            scratch_shapes=[pltpu.VMEM((8, chans), F32)],
        ),
        out_shape=outs,
        compiler_params=params(),
        cost_estimate=cost(8 * rows * width * chans, nbytes(grl, x, p_b, p_c, p_x, conv, w_b, w_c, w_x, w_out, *outs)),
        name="mixer_backward",
    )(base, grl, x, p_b, p_c, p_x, conv, next_grl, next_c, gain_one, taps, w_b, w_c, w_x, w_out)


def swap(value, step):
    count = lax.axis_size("tp")
    return lax.ppermute(value, "tp", [(i, i ^ step) for i in range(count)])


def shifted(value, steps):
    count = lax.axis_size("seq")
    return lax.ppermute(value, "seq", [(i, i + steps) for i in range(count) if 0 <= i + steps < count])


def others(value):
    count = lax.axis_size("tp")
    if count == 4:
        side = swap(value, 1)
        far = swap(value, 2)
        return [value, side, far, swap(side, 2)]
    every = lax.all_gather(value, "tp")
    me = lax.axis_index("tp")
    return [lax.dynamic_index_in_dim(every, me ^ j, 0, keepdims=False) for j in range(count)]


def scatter_sum(value):
    return lax.psum_scatter(value, "tp", scatter_dimension=0, tiled=True)


def gather(value):
    return lax.all_gather(value, "tp", axis=0, tiled=True)


def per_device(inputs, w_in, conv_w, w_out, norm_one, norm_two, w_gate, w_up, w_down, lengths, cotangent):
    rows, width = inputs.shape
    own = w_in.shape[2]
    units = w_gate.shape[1]
    slot = rows * lax.axis_size("seq") // SEQS
    tp = lax.axis_index("tp")
    quarter = rows // lax.axis_size("tp")
    start = lax.axis_index("seq") * rows
    base = start[None].astype(jnp.int32)

    w_in_all = others(jnp.concatenate([w_in[0], w_in[1], w_in[2]], axis=0))
    w_out_all = others(w_out)
    taps_all = others(jnp.concatenate([conv_w, jnp.zeros((13, own), BF16)], axis=0))
    w_b, w_c, w_x = (jnp.concatenate([w[i * width:(i + 1) * width] for w in w_in_all], axis=1) for i in range(3))
    w_o = jnp.concatenate(w_out_all, axis=0)
    taps = jnp.concatenate(taps_all, axis=1)[:8].astype(F32)
    gain_one = norm_one.astype(F32)[None, :]
    gain_two = norm_two.astype(F32)[None, :]

    place = start + jnp.arange(rows, dtype=jnp.int32)
    seq_of = place // slot
    limit = jnp.sum(jnp.where(seq_of[:, None] == jnp.arange(SEQS, dtype=jnp.int32)[None, :], lengths[None, :], 0), axis=1)
    real = (place - seq_of * slot < limit)[:, None]
    grad_low = jnp.where(real, cotangent, 0).astype(BF16)

    extra = -units % 128
    columns = lambda w: jnp.pad(w, ((0, 0), (0, extra)))
    w_gu = jnp.concatenate([columns(w_gate), columns(w_up)], axis=1)
    w_dn = jnp.pad(w_down, ((0, extra), (0, 0)))

    halo = shifted(inputs[rows - 16:], 1)
    h1, p_b, p_c, p_x, conv, gated, resid, h2 = mixer_forward(
        slot, base, inputs, halo, gain_one, gain_two, taps, w_b, w_c, w_x, w_o)
    next_c = shifted(p_c[:16], -1)

    out_part, back_part, activ, grads = ffn(h2, grad_low, w_gu, w_dn)
    d_hidden = scatter_sum(back_part).astype(F32)
    mine = lambda a: lax.dynamic_slice_in_dim(a, tp * quarter, quarter, 0)
    res = mine(resid)
    scale = rms_scale(res)
    normed = res * scale
    d_normed = d_hidden * gain_two
    g_norm_two = jnp.sum(d_hidden * normed, axis=0)
    g_res = mine(grad_low).astype(F32) + scale * (
        d_normed - normed * jnp.mean(d_normed * normed, axis=1, keepdims=True))
    grl = gather(g_res.astype(BF16))
    output = gather((res + scatter_sum(out_part).astype(F32)).astype(BF16))

    g_down = weight_grad(activ, grad_low)
    g_gu = weight_grad(h2, grads)

    next_grl = shifted(grl[:16], -1)
    grad_inputs, g_proj, g_conv, g_norm_one = mixer_backward(
        slot, own, base, grl, inputs, p_b, p_c, p_x, conv, next_grl, next_c, gain_one, taps, w_b, w_c, w_x, w_o)
    g_in = weight_grad(h1, g_proj)
    g_out = weight_grad(gated[:, :own], grl)

    big = lax.psum(tuple(a.astype(BF16) for a in (g_down, g_gu, g_in, g_out)), "seq")
    g_down, g_gu, g_in, g_out = (a.astype(F32) for a in big)
    g_conv, g_norm_one = lax.psum((g_conv[:3], g_norm_one[0]), "seq")
    g_norm_two = lax.psum(g_norm_two, ("seq", "tp"))
    padded = units + extra
    return (
        output,
        grad_inputs,
        jnp.stack([g_in[:, i * own:(i + 1) * own] for i in range(3)]),
        g_conv,
        g_out,
        g_norm_one,
        g_norm_two,
        g_gu[:, :units],
        g_gu[:, padded:padded + units],
        g_down[:units],
    )


def solution(mesh):
    tokens = P("seq", None)
    columns = P(None, "tp")
    lines = P("tp", None)
    stacked = P(None, None, "tp")
    return jax.shard_map(
        per_device,
        mesh=mesh,
        in_specs=(tokens, stacked, columns, lines, P(), P(), columns, columns, lines, P(), tokens),
        out_specs=(tokens, tokens, stacked, columns, lines, P(), P(), columns, columns, lines),
        check_vma=False,
    )
```

```python
import functools

import jax
import jax.numpy as jnp
from jax import lax
from jax.experimental import pallas as pl
from jax.experimental.pallas import tpu as pltpu
from jax.sharding import PartitionSpec as P

SEQS = 6
F32 = jnp.float32
BF16 = jnp.bfloat16
VMEM_LIMIT = 56 * 2**20
TILE = 256
CHUNKS = 3


def params():
    return pltpu.CompilerParams(vmem_limit_bytes=VMEM_LIMIT)


def cost(flops, moved):
    return pl.CostEstimate(flops=int(flops), bytes_accessed=int(moved), transcendentals=0)


def nbytes(*arrays):
    return sum(a.size * a.dtype.itemsize for a in arrays)


def shape(dims, dtype):
    return jax.ShapeDtypeStruct(dims, dtype)


def dot(left, right):
    return jnp.dot(left, right, preferred_element_type=F32)


def dot_nt(left, right):
    return lax.dot_general(left, right, (((1,), (1,)), ((), ())), preferred_element_type=F32)


def dot_tn(left, right):
    return lax.dot_general(left, right, (((0,), (0,)), ((), ())), preferred_element_type=F32)


def rms_scale(values):
    return lax.rsqrt(jnp.mean(values * values, axis=1, keepdims=True) + 1e-05)


def resident(array):
    zeros = (0,) * array.ndim
    return pl.BlockSpec(array.shape, lambda i, *_: zeros, pipeline_mode=pl.Buffered(1))


HALF = 128


def pack_half(w_in, conv_w, w_out):
    width = w_in.shape[1]
    out = w_out.reshape(HALF, width // HALF, HALF).transpose(1, 0, 2).reshape(width, HALF)
    taps = jnp.concatenate([conv_w, jnp.zeros((13, HALF), BF16)], axis=0)
    return jnp.concatenate([w_in.reshape(3 * width, HALF), out, taps], axis=0)


def group_arrays(group):
    kind, arrays = group
    return list(arrays) if kind == "whole" else [a for half in arrays for a in half]


def channels_of(group):
    kind, arrays = group
    return arrays[1].shape[0] if kind == "whole" else 2 * HALF


def copies(layout, refs, core, w_all, w_out, taps):
    width = w_all.shape[0]
    chans = w_out.shape[0]
    pairs, at, refs = [], 0, list(refs)
    for kind, size, arrays in layout:
        if kind == "whole":
            w_in, w_o, tap = (refs.pop(0) for _ in range(3))
            for i in range(3):
                pairs.append((w_in.at[i], w_all.at[:, pl.ds(i * chans + at, size)]))
            pairs.append((w_o, w_out.at[pl.ds(at, size), :]))
            pairs.append((tap, taps.at[:, pl.ds(at, size)]))
        else:
            for which, count in enumerate(arrays):
                parts = [refs.pop(0) for _ in range(count)]
                core_of = core if which == 0 else 1 - core
                place = at + core_of * HALF

                def rows(first, length):
                    if len(parts) == 1 or first < 2 * width:
                        return parts[0].at[pl.ds(first, length), :]
                    return parts[1].at[pl.ds(first - 2 * width, length), :]

                for i in range(3):
                    spot = pl.multiple_of(i * chans + place, HALF)
                    pairs.append((rows(i * width, width), w_all.at[:, pl.ds(spot, HALF)]))
                spot = pl.multiple_of(place, HALF)
                for j in range(width // HALF):
                    pairs.append((rows(3 * width + j * HALF, HALF), w_out.at[pl.ds(spot, HALF), pl.ds(j * HALF, HALF)]))
                pairs.append((rows(4 * width, 16), taps.at[:, pl.ds(spot, HALF)]))
        at += size
    return pairs


def layout_of(groups):
    return [(kind, channels_of((kind, arrays)), None if kind == "whole" else [len(h) for h in arrays])
            for kind, arrays in groups]


def copy_count(layout, width):
    per_half = 4 + width // HALF
    return sum(5 if kind == "whole" else 2 * per_half for kind, _, _ in layout)


def bring(pairs, sems):
    handles = [pltpu.make_async_copy(a, b, sems.at[k]) for k, (a, b) in enumerate(pairs)]
    for h in handles:
        h.start()
    for h in handles:
        h.wait()


def weight_scratch(width, chans, layout):
    return [
        pltpu.VMEM((width, 3 * chans), BF16),
        pltpu.VMEM((chans, width), BF16),
        pltpu.VMEM((16, chans), BF16),
        pltpu.SemaphoreType.DMA((copy_count(layout, width),)),
    ]


def layer_body(slot, own, layout, chunk_start, split, counts, info, lens, *refs):
    refs = list(refs)
    x, cot, halo, gain_one, gain_two = (refs.pop(0) for _ in range(5))
    weights = [refs.pop(0) for _ in range(counts[0])]
    w_gate, w_up, w_down = (refs.pop(0) for _ in range(3))
    del refs[:counts[1]]
    proj, gated, h1, h2, grad, activ, grads, resid = (refs.pop(0) for _ in range(8))
    forward = [refs.pop(0) for _ in range(4 if split else 1)]
    backward = [refs.pop(0) for _ in range(4 if split else 1)]
    w_all, w_out, taps, sems, w_gu, w_dn, more, carry = refs
    step = pl.program_id(0)
    rows, width = x.shape
    chans = w_out.shape[0]
    units = w_dn.shape[0]
    place = info[0] + chunk_start + step * rows

    def late():
        pairs = [(w_gate, w_gu.at[:, pl.ds(0, units)]), (w_up, w_gu.at[:, pl.ds(units, units)]), (w_down, w_dn)]
        return [pltpu.make_async_copy(a, b, more.at[k]) for k, (a, b) in enumerate(pairs)]

    def hidden(wide):
        return ((wide * rms_scale(wide)) * gain_one[...]).astype(BF16)

    @pl.when(step == 0)
    def _():
        early = [pltpu.make_async_copy(a, b, sems.at[k])
                 for k, (a, b) in enumerate(copies(layout, weights, info[1], w_all, w_out, taps))]
        for h in early:
            h.start()
        for h in late():
            h.start()
        for h in early:
            h.wait()
        for h in late():
            h.wait()
        before = dot(hidden(halo[...].astype(F32)), w_all[...])
        mixed = (before[:, :chans] * before[:, 2 * chans:]).astype(BF16).astype(F32)
        carry[...] = mixed[8:16]

    wide = x[...].astype(F32)
    low = hidden(wide)
    h1[...] = low
    every = dot(low, w_all[...])
    b, c, xx = (every[:, i * chans:(i + 1) * chans] for i in range(3))
    mixed = (b * xx).astype(BF16).astype(F32)
    before = jnp.where(lax.rem(place, slot) == 0, 0.0, carry[...])
    row = lax.broadcasted_iota(jnp.int32, mixed.shape, 0)
    one = jnp.where(row == 0, before[7:8], pltpu.roll(mixed, 1, 0))
    two = jnp.where(row == 0, before[6:7], jnp.where(row == 1, before[7:8], pltpu.roll(mixed, 2, 0)))
    carry[...] = mixed[rows - 8:]
    tap = taps[...].astype(F32)
    conved = tap[2:3] * mixed + tap[1:2] * one + tap[0:1] * two
    gate = (c * conved).astype(BF16)
    for i, part in enumerate((b, c, xx, conved)):
        proj[:, i * chans:(i + 1) * chans] = part.astype(BF16)
    gated[...] = gate[:, :own]
    res = wide + dot(gate, w_out[...])
    post = ((res * rms_scale(res)) * gain_two[...]).astype(BF16)
    h2[...] = post
    limit = lens[lax.div(place, slot)] - lax.rem(place, slot)
    line = lax.broadcasted_iota(jnp.int32, (rows, width), 0)
    low_grad = jnp.where(line < limit, cot[...].astype(F32), 0.0).astype(BF16)
    grad[...] = low_grad

    both = dot(post, w_gu[...])
    d_activ = dot_nt(low_grad, w_dn[...])
    pre = both[:, :units]
    up = both[:, units:]
    sig = 1.0 / (1.0 + jnp.exp(-pre))
    silu = pre * sig
    act = (silu * up).astype(BF16)
    g_gate = (d_activ * up * sig * (1.0 + pre * (1.0 - sig))).astype(BF16)
    g_up = (d_activ * silu).astype(BF16)
    activ[...] = act
    grads[:, :units] = g_gate
    grads[:, units:] = g_up
    back = dot_nt(grads[...], w_gu[...]).astype(BF16)
    out = dot(act, w_dn[...]).astype(BF16)
    if not split:
        forward[0][...] = out
        resid[...] = res
        backward[0][...] = back
        return
    far = lax.bitwise_xor(step, info[2])
    for j in range(4):
        @pl.when(far == j)
        def _():
            backward[j][...] = back
            forward[j][...] = out
            if j == 0:
                resid[...] = res


def layer(chunk, chunks, slot, own, info, lens, x, cot, halo, gain_one, gain_two, groups, w_gate, w_up, w_down, kept, after, tile, split):
    rows, width = x.shape
    layout = layout_of(groups)
    chans = sum(size for _, size, _ in layout)
    units = w_down.shape[0]
    weights = [a for g in groups for a in group_arrays(g)]
    steps = rows // chunks // tile
    row = lambda n: pl.BlockSpec((tile, n), lambda i, *_: (chunk * steps + i, 0))
    once = lambda n, at: pl.BlockSpec((tile, n), lambda i, *_: (at, 0))
    anywhere = pl.BlockSpec(memory_space=pl.ANY)
    outs = [shape((rows, 4 * chans), BF16), shape((rows, own), BF16), shape((rows, width), BF16),
            shape((rows, width), BF16), shape((rows, width), BF16), shape((rows, units), BF16), shape((rows, 2 * units), BF16)]
    specs = [row(s.shape[1]) for s in outs]
    part = pl.BlockSpec((tile, width), lambda i, *_: (i, 0))
    sums = shape((rows // chunks, width), BF16)
    if split:
        outs += [shape((chunks * tile, width), F32)] + [shape((chunks * tile, width), BF16)] * 4
        outs += [shape((tile, width), BF16)] * 4
        specs += [once(width, chunk)] * 5 + [once(width, 0)] * 4
    else:
        outs += [shape((rows, width), F32), sums, sums]
        specs += [row(width), part, part]
    ins = [x, cot, halo, gain_one, gain_two, *weights, w_gate, w_up, w_down, *kept, *after]
    result = pl.pallas_call(
        functools.partial(layer_body, slot, own, layout, chunk * steps * tile, split, (len(weights), len(kept) + len(after))),
        grid_spec=pltpu.PrefetchScalarGridSpec(
            num_scalar_prefetch=2,
            grid=(steps,),
            in_specs=[row(width), row(width)] + [resident(a) for a in (halo, gain_one, gain_two)]
            + [anywhere] * (len(weights) + 3 + len(kept) + len(after)),
            out_specs=specs,
            scratch_shapes=weight_scratch(width, chans, layout) + [
                pltpu.VMEM((width, 2 * units), BF16), pltpu.VMEM((units, width), BF16),
                pltpu.SemaphoreType.DMA((3,)), pltpu.VMEM((8, chans), F32)],
        ),
        out_shape=outs,
        input_output_aliases={2 + len(ins) - len(kept) - len(after) + k: k for k in range(len(kept))},
        compiler_params=params(),
        cost_estimate=cost(steps * tile * width * (8 * chans + 12 * units),
                           nbytes(x, cot, *outs[:7]) // chunks + nbytes(*weights, w_gate, w_up, w_down)),
        name="layer",
    )(info, lens, *ins)
    shared = 12 if split else 8
    return result[:shared], result[shared:]


def second_norm_body(info, d_own, d_side, d_far, d_corner, resid, grad, gain, out, g_norm):
    d_hidden = (d_own[...].astype(F32) + d_side[...].astype(F32)) + (d_far[...].astype(F32) + d_corner[...].astype(F32))
    res = resid[...]
    scale = rms_scale(res)
    normed = res * scale
    g_norm[...] = jnp.sum(d_hidden * normed, axis=0, keepdims=True)
    d_normed = d_hidden * gain[...]
    out[...] = (grad[...].astype(F32) + scale * (
        d_normed - normed * jnp.mean(d_normed * normed, axis=1, keepdims=True))).astype(BF16)


def second_norm(chunk, info, pieces, resid, grad, gain):
    block, width = pieces[0].shape
    same = pl.BlockSpec((block, width), lambda i, *_: (0, 0))
    return pl.pallas_call(
        second_norm_body,
        grid_spec=pltpu.PrefetchScalarGridSpec(
            num_scalar_prefetch=1,
            grid=(1,),
            in_specs=[same, same, same, same,
                      pl.BlockSpec((block, width), lambda i, info: (chunk, 0)),
                      pl.BlockSpec((block, width), lambda i, info: (4 * chunk + info[2], 0)),
                      resident(gain)],
            out_specs=[same, pl.BlockSpec((1, width), lambda i, *_: (0, 0))],
        ),
        out_shape=[shape((block, width), BF16), shape((1, width), F32)],
        compiler_params=params(),
        cost_estimate=cost(0, 14 * block * width),
        name="second_norm",
    )(info, *pieces, resid, grad, gain)


def place_body(info, own, side, far, left, right, *refs):
    target = refs[-1]
    j = pl.program_id(0) % 4
    for k, source in enumerate((own, side, far)):
        @pl.when(j == k)
        def _():
            target[...] = source[...]

    @pl.when(j == 3)
    def _():
        target[:, :left.shape[1]] = left[...]
        target[:, left.shape[1]:] = right[...]


def place(first, chunks, info, pieces, rows, into, corner=0):
    width = pieces[0].shape[1]
    block = pieces[0].shape[0] // chunks
    kept = [] if into is None else [into]
    at = [0, 0, 0, corner, corner]
    return pl.pallas_call(
        place_body,
        grid_spec=pltpu.PrefetchScalarGridSpec(
            num_scalar_prefetch=1,
            grid=(4 * chunks,),
            in_specs=[pl.BlockSpec((block, p.shape[1]), lambda i, *_, k=k: (k + i // 4, 0)) for p, k in zip(pieces, at)]
            + [pl.BlockSpec(memory_space=pl.ANY)] * len(kept),
            out_specs=pl.BlockSpec((block, width), lambda i, info: (4 * (first + i // 4) + lax.bitwise_xor(i % 4, info[2]), 0)),
        ),
        out_shape=shape((rows, width), BF16),
        input_output_aliases={6: 0} if kept else {},
        compiler_params=params(),
        cost_estimate=cost(0, 2 * nbytes(*pieces)),
        name="place",
    )(info, *pieces, *kept)


def weight_grad_body(left, right, *refs):
    out = refs[-1]
    out[...] = dot_tn(left[...], right[...]).astype(out.dtype)


def weight_grad(left, right, after=(), first=0, wide=None, dtype=F32):
    rows, high = left.shape
    wide = wide or right.shape[1]
    tile = next(t for t in (768, 640, 512, 384, 256, 128) if wide % t == 0)
    return pl.pallas_call(
        weight_grad_body,
        grid=(wide // tile,),
        in_specs=[resident(left), pl.BlockSpec((rows, tile), lambda i: (0, first // tile + i))]
        + [pl.BlockSpec(memory_space=pl.ANY)] * len(after),
        out_specs=pl.BlockSpec((high, tile), lambda i: (0, i)),
        out_shape=shape((high, wide), dtype),
        compiler_params=params(),
        cost_estimate=cost(2 * rows * high * wide, nbytes(left) + 2 * rows * wide + 4 * high * wide),
        name="weight_grad",
    )(left, right, *after)


def conv_backward(slot, info, total, d_gated, c, conved, taps, carry):
    step = pl.program_id(0)
    rows = d_gated.shape[0]
    d_conv = d_gated * c[...].astype(F32)
    g_c = (d_gated * conved[...].astype(F32)).astype(BF16)
    fresh = lax.rem(info[0] + (total - step) * rows, slot) == 0
    after = jnp.where(fresh, 0.0, carry[...])
    row = lax.broadcasted_iota(jnp.int32, d_conv.shape, 0)
    one = jnp.where(row == rows - 1, after[0:1], pltpu.roll(d_conv, rows - 1, 0))
    two = jnp.where(row == rows - 2, after[0:1], jnp.where(row == rows - 1, after[1:2], pltpu.roll(d_conv, rows - 2, 0)))
    carry[...] = d_conv[0:8]
    tap = taps[...].astype(F32)
    return d_conv, one, two, g_c, tap[2:3] * d_conv + tap[1:2] * one + tap[0:1] * two


def own_backward_body(slot, info, grl, p_b, p_c, p_x, conved, next_grl, next_c, w_out, taps, *refs):
    g_proj, g_conv, carry = refs[-3:]

    @pl.when(pl.program_id(0) == 0)
    def _():
        carry[...] = (dot_nt(next_grl[...], w_out[...]) * next_c[...].astype(F32))[0:8]
        g_conv[...] = jnp.zeros_like(g_conv)

    own = w_out.shape[0]
    d_conv, one, two, g_c, d_mixed = conv_backward(slot, info, pl.num_programs(0), dot_nt(grl[...], w_out[...]), p_c, conved, taps, carry)
    b = p_b[...].astype(F32)
    xx = p_x[...].astype(F32)
    mixed = (b * xx).astype(BF16).astype(F32)
    g_proj[:, :own] = (d_mixed * xx).astype(BF16)
    g_proj[:, own:2 * own] = g_c
    g_proj[:, 2 * own:] = (d_mixed * b).astype(BF16)
    for k, values in enumerate((two, one, d_conv)):
        g_conv[k:k + 1] += jnp.sum(values * mixed, axis=0, keepdims=True)


def own_backward(slot, info, grl, proj, next_grl, next_c, w_out, taps, after=(), tile=512):
    rows, width = grl.shape
    own = w_out.shape[0]
    groups = proj.shape[1] // 4 // own
    steps = rows // tile
    row = lambda n, at=0: pl.BlockSpec((tile, n), lambda i, *_: (steps - 1 - i, at))
    outs = [shape((rows, 3 * own), BF16), shape((8, own), F32)]
    ins = [grl, proj, proj, proj, proj, next_grl, next_c, w_out, taps]
    return pl.pallas_call(
        functools.partial(own_backward_body, slot),
        grid_spec=pltpu.PrefetchScalarGridSpec(
            num_scalar_prefetch=1,
            grid=(steps,),
            in_specs=[row(width)] + [row(own, k * groups) for k in range(4)] + [resident(a) for a in ins[5:]]
            + [pl.BlockSpec(memory_space=pl.ANY)] * len(after),
            out_specs=[row(3 * own), pl.BlockSpec((8, own), lambda i, *_: (0, 0))],
            scratch_shapes=[pltpu.VMEM((8, own), F32)],
        ),
        out_shape=outs,
        compiler_params=params(),
        cost_estimate=cost(2 * rows * width * own, nbytes(grl, *outs) + nbytes(proj) // groups),
        name="own_backward",
    )(info, *ins, *after)


def mixer_backward_body(slot, layout, count, total, begun, info, grl, x, p_b, p_c, p_x, conved, next_grl, next_c, gain_one, *refs):
    weights = refs[:count]
    g_in, g_norm, rest, w_all, w_out, taps, sems, carry, held = refs[-9:]
    step = pl.program_id(0)
    chans = w_out.shape[0]

    @pl.when(step == 0)
    def _():
        bring(copies(layout, weights, info[1], w_all, w_out, taps), sems)
        if begun:
            carry[...] = refs[count][...]
        else:
            carry[...] = (dot_nt(next_grl[...], w_out[...]) * next_c[...].astype(F32))[0:8]
        g_norm[...] = jnp.zeros_like(g_norm)

    _, _, _, g_c, d_mixed = conv_backward(slot, info, total, dot_nt(grl[...], w_out[...]), p_c, conved, taps, carry)
    rest[...] = carry[...]
    held[:, :chans] = (d_mixed * p_x[...].astype(F32)).astype(BF16)
    held[:, chans:2 * chans] = g_c
    held[:, 2 * chans:] = (d_mixed * p_b[...].astype(F32)).astype(BF16)
    d_hidden = dot_nt(held[...], w_all[...])
    wide = x[...].astype(F32)
    scale = rms_scale(wide)
    normed = wide * scale
    g_norm[0:1] += jnp.sum(d_hidden * normed, axis=0, keepdims=True)
    d_normed = d_hidden * gain_one[...]
    g_in[...] = grl[...].astype(F32) + scale * (
        d_normed - normed * jnp.mean(d_normed * normed, axis=1, keepdims=True))


def mixer_backward(slot, info, grl, x, proj, next_grl, next_c, gain_one, groups, after=(), part=0, parts=1, kept=(), tile=512):
    rows, width = x.shape
    layout = layout_of(groups)
    chans = sum(size for _, size, _ in layout)
    weights = [a for g in groups for a in group_arrays(g)]
    steps = rows // tile // parts
    total = rows // tile - part * steps
    row = lambda n, at=0: pl.BlockSpec((tile, n), lambda i, *_: (total - 1 - i, at))
    outs = [shape((rows, width), F32), shape((8, width), F32), shape((8, chans), F32)]
    fixed = lambda n: pl.BlockSpec((8, n), lambda i, *_: (0, 0))
    ins = [grl, x, proj, proj, proj, proj, next_grl, next_c, gain_one, *weights, *kept]
    anywhere = pl.BlockSpec(memory_space=pl.ANY)
    return pl.pallas_call(
        functools.partial(mixer_backward_body, slot, layout, len(weights), total, bool(kept)),
        grid_spec=pltpu.PrefetchScalarGridSpec(
            num_scalar_prefetch=1,
            grid=(steps,),
            in_specs=[row(width), row(width)] + [row(chans, k) for k in range(4)]
            + [resident(a) for a in (next_grl, next_c, gain_one)] + [anywhere] * len(weights)
            + ([resident(kept[0]), anywhere] if kept else []) + [anywhere] * len(after),
            out_specs=[row(width), fixed(width), fixed(chans)],
            scratch_shapes=weight_scratch(width, chans, layout)
            + [pltpu.VMEM((8, chans), F32), pltpu.VMEM((tile, 3 * chans), BF16)],
        ),
        out_shape=outs,
        input_output_aliases={len(ins): 0} if kept else {},
        compiler_params=params(),
        cost_estimate=cost(8 * rows * width * chans // parts, nbytes(grl, x, proj, *outs) // parts + nbytes(*weights)),
        name="mixer_backward",
    )(info, *ins, *after)


def swap(value, step):
    count = lax.axis_size("tp")
    return lax.ppermute(value, "tp", [(i, i ^ step) for i in range(count)])


def swap_seq(value, step):
    count = lax.axis_size("seq")
    return lax.ppermute(value, "seq", [(i, i ^ step) for i in range(count)])


def shifted(value, steps):
    count = lax.axis_size("seq")
    return lax.ppermute(value, "seq", [(i, i + steps) for i in range(count) if 0 <= i + steps < count])


def weight_groups(w_in, conv_w, w_out, core, tp):
    own_taps = jnp.concatenate([conv_w, jnp.zeros((13, conv_w.shape[1]), BF16)], axis=0)
    own = ("whole", [w_in, w_out, own_taps])
    width = w_in.shape[1]
    if lax.axis_size("tp") == 4 and w_out.shape[0] == 2 * HALF:
        cut = lambda a, dim: lax.dynamic_slice_in_dim(a, core * HALF, HALF, dim)
        half = pack_half(cut(w_in, 2), cut(conv_w, 1), cut(w_out, 0))
        side, far = swap(half, 1), swap(half, 2)
        low, high = swap(side[:2 * width], 2), swap(far[2 * width:], 1)
        pairs = [("halves", [[side], [swap_seq(side, 1)]]), ("halves", [[far], [swap_seq(far, 1)]])]
        corner = ("halves", [[low, high], [swap_seq(low, 1), swap_seq(high, 1)]])
        return [own, *pairs, corner]
    every = [lax.all_gather(a, "tp") for a in own[1]]
    take = lambda a, j: lax.dynamic_index_in_dim(a, tp ^ j, 0, keepdims=False)
    return [own] + [("whole", [take(a, j) for a in every]) for j in range(1, lax.axis_size("tp"))]


def exchange(blocks):
    return [blocks[0]] + [swap(blocks[j], j) for j in (3, 1, 2)]


def to_sides(own):
    return [swap(own, 1), swap(own, 2)]


def corners(sides):
    half = sides[0][0].shape[1] // 2
    low = [far[:, :half] for _, far in sides]
    high = [side[:, half:] for side, _ in sides]
    join = lambda parts: parts[0] if len(parts) == 1 else jnp.concatenate(parts, axis=0)
    return [swap(join(low), 1), swap(join(high), 2)]


class SeqSum:
    def __init__(self, value):
        seq = lax.axis_index("seq")
        self.core = seq & 1
        line = seq >> 1
        self.keep = (line & 1) ^ (line >> 1)
        self.rows = value.shape[0]
        self.value = value

    def cut(self, array, which, count):
        size = self.rows // count
        return lax.dynamic_slice_in_dim(array, which * size, size, 0)

    def pair(self):
        self.sent = swap_seq(self.cut(self.value, 1 - self.core, 2).astype(BF16), 1)

    def near(self):
        self.value = self.cut(self.value, self.core, 2) + self.sent.astype(F32)
        self.sent = swap_seq(self.cut(self.value, 1 - self.keep, 4).astype(BF16), 2)

    def cross(self):
        self.value = (self.cut(self.value, self.keep, 4) + self.sent.astype(F32)).astype(BF16)
        self.sent = swap_seq(self.value, 6)

    def back(self):
        self.value = (self.value.astype(F32) + self.sent.astype(F32)).astype(BF16)
        self.sent = swap_seq(self.value, 2)

    def share(self):
        first = self.keep == 0
        self.value = jnp.concatenate([jnp.where(first, self.value, self.sent), jnp.where(first, self.sent, self.value)], axis=0)
        self.sent = swap_seq(self.value, 1)

    def result(self):
        first = self.core == 0
        return jnp.concatenate(
            [jnp.where(first, self.value, self.sent), jnp.where(first, self.sent, self.value)], axis=0).astype(F32)

    def state(self):
        return self.value, self.sent

    def put(self, state):
        self.value, self.sent = state


def seq_sum(value):
    return lax.psum(value.astype(BF16), "seq").astype(F32)


def small_sum(value):
    if lax.axis_size("seq") != 8:
        return lax.psum(value, "seq")
    for step in (1, 2, 6):
        value = value + swap_seq(value, step)
    return value


def per_device(inputs, w_in, conv_w, w_out, norm_one, norm_two, w_gate, w_up, w_down, lengths, cotangent):
    rows, width = inputs.shape
    own = w_in.shape[2]
    units = w_gate.shape[1]
    slot = rows * lax.axis_size("seq") // SEQS
    group = lax.axis_size("tp")
    tp = lax.axis_index("tp")
    seq = lax.axis_index("seq")
    core = seq & 1
    info = jnp.stack([seq * rows, core, tp]).astype(jnp.int32)
    chunk = rows // CHUNKS
    block = chunk // group
    split = group == 4

    halo = shifted(inputs[rows - 16:], 1)
    groups = weight_groups(w_in, conv_w, w_out, core, tp)
    gain_one = norm_one.astype(F32)[None, :]
    gain_two = norm_two.astype(F32)[None, :]
    extra = -units % 128
    columns = lambda w: jnp.pad(w, ((0, 0), (0, extra)))
    w_gate, w_up, w_down = columns(w_gate), columns(w_up), jnp.pad(w_down, ((0, extra), (0, 0)))
    padded = units + extra

    scatter = lambda a: lax.psum_scatter(a, "tp", scatter_dimension=0, tiled=True)
    gather = lambda a: lax.all_gather(a.astype(BF16), "tp", axis=0, tiled=True)
    tie = lax.optimization_barrier

    def chunk_layer(k, kept, after=()):
        before = halo if k == 0 else inputs[k * chunk - 16:k * chunk]
        return layer(k, CHUNKS, slot, own, info, lengths, inputs, cotangent, before, gain_one, gain_two, groups,
                     w_gate, w_up, w_down, kept, after, block if split else TILE, split)

    if split and lax.axis_size("seq") == 8:
        kept, blocks0 = chunk_layer(0, [])
        terms0 = exchange(blocks0)
        kept, blocks1 = chunk_layer(1, kept)
        kept, blocks1, terms0 = tie((kept, blocks1, terms0))

        share0, norm0 = second_norm(0, info, terms0, kept[7], kept[4], gain_two)
        terms1 = exchange(blocks1)
        sides0 = to_sides(share0)
        kept, blocks2 = chunk_layer(2, kept, [share0])
        kept, blocks2, sides0, terms1 = tie((kept, blocks2, sides0, terms1))

        proj, gated, h1, h2, grad_low, activ, grads, resid = kept[:8]
        terms2 = exchange(blocks2)
        share1, norm1 = second_norm(1, info, terms1, resid, grad_low, gain_two)
        sides1 = to_sides(share1)
        split_at = 2 * padded * 2 // 3
        g_first = weight_grad(h2, grads, [share1], 0, split_at)
        g_first, terms2, activ, share1, grads = tie((g_first, terms2, activ, share1, grads))

        first = SeqSum(g_first)
        first.pair()
        share2, norm2 = second_norm(2, info, terms2, resid, grad_low, gain_two)
        sides2 = to_sides(share2)
        g_down = weight_grad(activ, grad_low, [share2], dtype=BF16)
        g_down, grads, sides1, state = tie((g_down, grads, sides1, first.state()))

        first.put(state)
        first.near()
        corner01 = corners([sides0, sides1])
        next_c = shifted(proj[:16, width:2 * width], -1)
        g_second = weight_grad(h2, grads, [first.value], split_at, 2 * padded - split_at, BF16)
        g_second, corner01, sides2, next_c, state, forward = tie(
            (g_second, corner01, sides2, next_c, first.state(), kept[8:12]))

        first.put(state)
        first.cross()
        g_down, g_second = lax.psum((g_down, g_second), "seq")
        corner2 = corners([sides2])
        grl = place(0, 1, info, [share0, *sides0, *corner01], rows, None)
        next_grl = shifted(grl[:16], -1)
        grl = place(1, 1, info, [share1, *sides1, *corner01], rows, grl, 1)
        grl, next_grl, corner2, forward = tie((grl, next_grl, corner2, forward))

        terms = exchange(forward)
        grl = place(2, 1, info, [share2, *sides2, *corner2], rows, grl)
        g_proj, g_conv = own_backward(slot, info, grl, proj, next_grl, next_c[:, :own], w_out, groups[0][1][2])
        g_in = weight_grad(h1, g_proj)
        g_in, terms[1], state = tie((g_in, terms[1], first.state()))

        first.put(state)
        first.back()
        tail_in = SeqSum(jnp.concatenate([g_in, jnp.pad(g_conv[:3].reshape(1, -1), ((0, 15), (0, 0)))], axis=0))
        tail_in.pair()
        g_out = weight_grad(gated, grl, [tail_in.value])
        g_out, state = tie((g_out, tail_in.state()))

        tail_in.put(state)
        tail_in.near()
        tail_out = SeqSum(g_out)
        tail_out.pair()
        g_norm_two = norm0 + norm1 + norm2
        g_norm_two = g_norm_two + swap(g_norm_two, 1)
        back = lambda k, kept, after: mixer_backward(
            slot, info, grl, inputs, proj, next_grl, next_c, gain_one, groups, after, k, 2, kept)
        grad_inputs, norm_late, rest = back(0, (), [tail_in.value])
        grad_inputs, norm_late, rest, terms, g_norm_two, state, state2, state3 = tie((
            grad_inputs, norm_late, rest, terms, g_norm_two, tail_in.state(), tail_out.state(), first.state()))

        tail_in.put(state)
        tail_out.put(state2)
        first.put(state3)
        final = (resid + sum(t.astype(F32) for t in terms)).astype(BF16)
        sides = to_sides(final)
        tail_in.cross()
        tail_out.near()
        grad_inputs, norm_early, _ = back(1, (rest, grad_inputs), [tail_in.value, tail_out.value, final])
        grad_inputs, norm_early, sides, g_down, g_second, state, state2, state3 = tie((
            grad_inputs, norm_early, sides, g_down, g_second, tail_in.state(), tail_out.state(), first.state()))

        tail_in.put(state)
        tail_out.put(state2)
        first.put(state3)
        corner = corners([sides])
        first.share()
        tail_in.back()
        tail_out.cross()
        g_norm_two = g_norm_two + swap(g_norm_two, 2)
        norms = small_sum(jnp.concatenate([norm_early[:1] + norm_late[:1], g_norm_two], axis=0))
        g_norm_one, g_norm_two = norms[0], norms[1]
        output = place(0, CHUNKS, info, [final, *sides, *corner], rows, None)
        tail_in.share()
        tail_out.back()
        tail_out.share()
        g_first = first.result()
        g_gu = jnp.concatenate([g_first, g_second.astype(F32)], axis=1)
        g_down = g_down.astype(F32)
        g_out = tail_out.result()
        g_in = tail_in.result()
        g_conv = g_in[width].reshape(3, own)
    else:
        kept, finals, shares, g_norm_two = [], [], [], 0.0
        cut = lambda a, k: lax.dynamic_slice_in_dim(a, k * chunk + tp * block, block, 0)
        whole = lambda blocks: blocks[0] if not split else jnp.concatenate(
            [lax.dynamic_index_in_dim(jnp.stack(blocks), tp ^ j, 0, keepdims=False) for j in range(4)], axis=0)
        for k in range(CHUNKS):
            kept, blocks = chunk_layer(k, kept)
            terms = kept[8:12] if split else blocks[:1]
            terms = [t[k * block:(k + 1) * block] for t in terms] if split else terms
            d_hidden = scatter(whole(blocks if split else blocks[1:])).astype(F32)
            res = kept[7][k * block:(k + 1) * block] if split else cut(kept[7], k)
            finals.append(gather(res + scatter(whole(terms)).astype(F32)))
            scale = rms_scale(res)
            normed = res * scale
            d_normed = d_hidden * gain_two
            g_norm_two += jnp.sum(d_hidden * normed, axis=0)
            shares.append(gather(cut(kept[4], k).astype(F32) + scale * (
                d_normed - normed * jnp.mean(d_normed * normed, axis=1, keepdims=True))))
        proj, gated, h1, h2, grad_low, activ, grads, resid = kept[:8]
        grl = jnp.concatenate(shares, axis=0)
        output = jnp.concatenate(finals, axis=0)
        g_norm_two = lax.psum(g_norm_two, "tp")
        next_c = shifted(proj[:16, width:2 * width], -1)
        next_grl = shifted(grl[:16], -1)
        g_proj, g_conv = own_backward(slot, info, grl, proj, next_grl, next_c[:, :own], w_out, groups[0][1][2])
        grad_inputs, g_norm_one, _ = mixer_backward(slot, info, grl, inputs, proj, next_grl, next_c, gain_one, groups)
        g_norm_one = small_sum(g_norm_one[0])
        g_down = seq_sum(weight_grad(activ, grad_low))
        g_gu = seq_sum(weight_grad(h2, grads))
        g_out = seq_sum(weight_grad(gated, grl))
        g_in = seq_sum(weight_grad(h1, g_proj))
        g_conv = lax.psum(g_conv[:3], "seq")
        g_norm_two = lax.psum(g_norm_two, "seq")
    g_in = g_in[:width]
    return (
        output,
        grad_inputs,
        jnp.stack([g_in[:, i * own:(i + 1) * own] for i in range(3)]),
        g_conv,
        g_out,
        g_norm_one,
        g_norm_two,
        g_gu[:, :units],
        g_gu[:, padded:padded + units],
        g_down[:units],
    )


def solution(mesh):
    tokens = P("seq", None)
    columns = P(None, "tp")
    lines = P("tp", None)
    stacked = P(None, None, "tp")
    return jax.shard_map(
        per_device,
        mesh=mesh,
        in_specs=(tokens, stacked, columns, lines, P(), P(), columns, columns, lines, P(), tokens),
        out_specs=(tokens, tokens, stacked, columns, lines, P(), P(), columns, columns, lines),
        check_vma=False,
    )
```

```python
import functools

import jax
import jax.numpy as jnp
from jax import lax
from jax.experimental import pallas as pl
from jax.experimental.pallas import tpu as pltpu
from jax.sharding import PartitionSpec as P

SEQS = 6
F32 = jnp.float32
BF16 = jnp.bfloat16
VMEM_LIMIT = 56 * 2**20
TILE = 256
CHUNKS = 3


def params():
    return pltpu.CompilerParams(vmem_limit_bytes=VMEM_LIMIT)


def cost(flops, moved):
    return pl.CostEstimate(flops=int(flops), bytes_accessed=int(moved), transcendentals=0)


def nbytes(*arrays):
    return sum(a.size * a.dtype.itemsize for a in arrays)


def shape(dims, dtype):
    return jax.ShapeDtypeStruct(dims, dtype)


def dot(left, right):
    return jnp.dot(left, right, preferred_element_type=F32)


def dot_nt(left, right):
    return lax.dot_general(left, right, (((1,), (1,)), ((), ())), preferred_element_type=F32)


def dot_tn(left, right):
    return lax.dot_general(left, right, (((0,), (0,)), ((), ())), preferred_element_type=F32)


def rms_scale(values):
    return lax.rsqrt(jnp.mean(values * values, axis=1, keepdims=True) + 1e-05)


def resident(array):
    zeros = (0,) * array.ndim
    return pl.BlockSpec(array.shape, lambda i, *_: zeros, pipeline_mode=pl.Buffered(1))


HALF = 128


def pack_half(w_in, conv_w, w_out):
    width = w_in.shape[1]
    out = w_out.reshape(HALF, width // HALF, HALF).transpose(1, 0, 2).reshape(width, HALF)
    taps = jnp.concatenate([conv_w, jnp.zeros((13, HALF), BF16)], axis=0)
    return jnp.concatenate([w_in.reshape(3 * width, HALF), out, taps], axis=0)


def group_arrays(group):
    kind, arrays = group
    return list(arrays) if kind == "whole" else [a for half in arrays for a in half]


def channels_of(group):
    kind, arrays = group
    return arrays[1].shape[0] if kind == "whole" else 2 * HALF


def copies(layout, refs, core, w_all, w_out, taps):
    width = w_all.shape[0]
    chans = w_out.shape[0]
    pairs, at, refs = [], 0, list(refs)
    for kind, size, arrays in layout:
        if kind == "whole":
            w_in, w_o, tap = (refs.pop(0) for _ in range(3))
            for i in range(3):
                pairs.append((w_in.at[i], w_all.at[:, pl.ds(i * chans + at, size)]))
            pairs.append((w_o, w_out.at[pl.ds(at, size), :]))
            pairs.append((tap, taps.at[:, pl.ds(at, size)]))
        else:
            for which, count in enumerate(arrays):
                parts = [refs.pop(0) for _ in range(count)]
                core_of = core if which == 0 else 1 - core
                place = at + core_of * HALF

                def rows(first, length):
                    if len(parts) == 1 or first < 2 * width:
                        return parts[0].at[pl.ds(first, length), :]
                    return parts[1].at[pl.ds(first - 2 * width, length), :]

                for i in range(3):
                    spot = pl.multiple_of(i * chans + place, HALF)
                    pairs.append((rows(i * width, width), w_all.at[:, pl.ds(spot, HALF)]))
                spot = pl.multiple_of(place, HALF)
                for j in range(width // HALF):
                    pairs.append((rows(3 * width + j * HALF, HALF), w_out.at[pl.ds(spot, HALF), pl.ds(j * HALF, HALF)]))
                pairs.append((rows(4 * width, 16), taps.at[:, pl.ds(spot, HALF)]))
        at += size
    return pairs


def layout_of(groups):
    return [(kind, channels_of((kind, arrays)), None if kind == "whole" else [len(h) for h in arrays])
            for kind, arrays in groups]


def copy_count(layout, width):
    per_half = 4 + width // HALF
    return sum(5 if kind == "whole" else 2 * per_half for kind, _, _ in layout)


def bring(pairs, sems):
    handles = [pltpu.make_async_copy(a, b, sems.at[k]) for k, (a, b) in enumerate(pairs)]
    for h in handles:
        h.start()
    for h in handles:
        h.wait()


def weight_scratch(width, chans, layout):
    return [
        pltpu.VMEM((width, 3 * chans), BF16),
        pltpu.VMEM((chans, width), BF16),
        pltpu.VMEM((16, chans), BF16),
        pltpu.SemaphoreType.DMA((copy_count(layout, width),)),
    ]


def layer_body(slot, own, layout, chunk_start, split, counts, info, lens, *refs):
    refs = list(refs)
    x, cot, halo, gain_one, gain_two = (refs.pop(0) for _ in range(5))
    weights = [refs.pop(0) for _ in range(counts[0])]
    w_gate, w_up, w_down = (refs.pop(0) for _ in range(3))
    del refs[:counts[1]]
    proj, gated, h1, h2, grad, activ, grads, resid = (refs.pop(0) for _ in range(8))
    forward = [refs.pop(0) for _ in range(4 if split else 1)]
    backward = [refs.pop(0) for _ in range(4 if split else 1)]
    w_all, w_out, taps, sems, w_gu, w_dn, more, carry = refs
    step = pl.program_id(0)
    rows, width = x.shape
    chans = w_out.shape[0]
    units = w_dn.shape[0]
    place = info[0] + chunk_start + step * rows

    def late():
        pairs = [(w_gate, w_gu.at[:, pl.ds(0, units)]), (w_up, w_gu.at[:, pl.ds(units, units)]), (w_down, w_dn)]
        return [pltpu.make_async_copy(a, b, more.at[k]) for k, (a, b) in enumerate(pairs)]

    def hidden(wide):
        return ((wide * rms_scale(wide)) * gain_one[...]).astype(BF16)

    @pl.when(step == 0)
    def _():
        early = [pltpu.make_async_copy(a, b, sems.at[k])
                 for k, (a, b) in enumerate(copies(layout, weights, info[1], w_all, w_out, taps))]
        for h in early:
            h.start()
        for h in late():
            h.start()
        for h in early:
            h.wait()
        for h in late():
            h.wait()
        before = dot(hidden(halo[...].astype(F32)), w_all[...])
        mixed = (before[:, :chans] * before[:, 2 * chans:]).astype(BF16).astype(F32)
        carry[...] = mixed[8:16]

    wide = x[...].astype(F32)
    low = hidden(wide)
    h1[...] = low
    every = dot(low, w_all[...])
    b, c, xx = (every[:, i * chans:(i + 1) * chans] for i in range(3))
    mixed = (b * xx).astype(BF16).astype(F32)
    before = jnp.where(lax.rem(place, slot) == 0, 0.0, carry[...])
    row = lax.broadcasted_iota(jnp.int32, mixed.shape, 0)
    one = jnp.where(row == 0, before[7:8], pltpu.roll(mixed, 1, 0))
    two = jnp.where(row == 0, before[6:7], jnp.where(row == 1, before[7:8], pltpu.roll(mixed, 2, 0)))
    carry[...] = mixed[rows - 8:]
    tap = taps[...].astype(F32)
    conved = tap[2:3] * mixed + tap[1:2] * one + tap[0:1] * two
    gate = (c * conved).astype(BF16)
    for i, part in enumerate((b, c, xx, conved)):
        proj[:, i * chans:(i + 1) * chans] = part.astype(BF16)
    gated[...] = gate[:, :own]
    res = wide + dot(gate, w_out[...])
    post = ((res * rms_scale(res)) * gain_two[...]).astype(BF16)
    h2[...] = post
    limit = lens[lax.div(place, slot)] - lax.rem(place, slot)
    line = lax.broadcasted_iota(jnp.int32, (rows, width), 0)
    low_grad = jnp.where(line < limit, cot[...].astype(F32), 0.0).astype(BF16)
    grad[...] = low_grad

    both = dot(post, w_gu[...])
    d_activ = dot_nt(low_grad, w_dn[...])
    pre = both[:, :units]
    up = both[:, units:]
    sig = 1.0 / (1.0 + jnp.exp(-pre))
    silu = pre * sig
    act = (silu * up).astype(BF16)
    g_gate = (d_activ * up * sig * (1.0 + pre * (1.0 - sig))).astype(BF16)
    g_up = (d_activ * silu).astype(BF16)
    activ[...] = act
    grads[:, :units] = g_gate
    grads[:, units:] = g_up
    back = dot_nt(grads[...], w_gu[...]).astype(BF16)
    out = dot(act, w_dn[...]).astype(BF16)
    if not split:
        forward[0][...] = out
        resid[...] = res
        backward[0][...] = back
        return
    far = lax.bitwise_xor(step, info[2])
    for j in range(4):
        @pl.when(far == j)
        def _():
            backward[j][...] = back
            forward[j][...] = out
            if j == 0:
                resid[...] = res


def layer(chunk, chunks, slot, own, info, lens, x, cot, halo, gain_one, gain_two, groups, w_gate, w_up, w_down, kept, after, tile, split):
    rows, width = x.shape
    layout = layout_of(groups)
    chans = sum(size for _, size, _ in layout)
    units = w_down.shape[0]
    weights = [a for g in groups for a in group_arrays(g)]
    steps = rows // chunks // tile
    row = lambda n: pl.BlockSpec((tile, n), lambda i, *_: (chunk * steps + i, 0))
    once = lambda n, at: pl.BlockSpec((tile, n), lambda i, *_: (at, 0))
    anywhere = pl.BlockSpec(memory_space=pl.ANY)
    outs = [shape((rows, 4 * chans), BF16), shape((rows, own), BF16), shape((rows, width), BF16),
            shape((rows, width), BF16), shape((rows, width), BF16), shape((rows, units), BF16), shape((rows, 2 * units), BF16)]
    specs = [row(s.shape[1]) for s in outs]
    part = pl.BlockSpec((tile, width), lambda i, *_: (i, 0))
    sums = shape((rows // chunks, width), BF16)
    if split:
        outs += [shape((chunks * tile, width), F32)] + [shape((chunks * tile, width), BF16)] * 4
        outs += [shape((tile, width), BF16)] * 4
        specs += [once(width, chunk)] * 5 + [once(width, 0)] * 4
    else:
        outs += [shape((rows, width), F32), sums, sums]
        specs += [row(width), part, part]
    ins = [x, cot, halo, gain_one, gain_two, *weights, w_gate, w_up, w_down, *kept, *after]
    result = pl.pallas_call(
        functools.partial(layer_body, slot, own, layout, chunk * steps * tile, split, (len(weights), len(kept) + len(after))),
        grid_spec=pltpu.PrefetchScalarGridSpec(
            num_scalar_prefetch=2,
            grid=(steps,),
            in_specs=[row(width), row(width)] + [resident(a) for a in (halo, gain_one, gain_two)]
            + [anywhere] * (len(weights) + 3 + len(kept) + len(after)),
            out_specs=specs,
            scratch_shapes=weight_scratch(width, chans, layout) + [
                pltpu.VMEM((width, 2 * units), BF16), pltpu.VMEM((units, width), BF16),
                pltpu.SemaphoreType.DMA((3,)), pltpu.VMEM((8, chans), F32)],
        ),
        out_shape=outs,
        input_output_aliases={2 + len(ins) - len(kept) - len(after) + k: k for k in range(len(kept))},
        compiler_params=params(),
        cost_estimate=cost(steps * tile * width * (8 * chans + 12 * units),
                           nbytes(x, cot, *outs[:7]) // chunks + nbytes(*weights, w_gate, w_up, w_down)),
        name="layer",
    )(info, lens, *ins)
    shared = 12 if split else 8
    return result[:shared], result[shared:]


def second_norm_body(info, d_own, d_side, d_far, d_corner, resid, grad, gain, out, g_norm):
    d_hidden = (d_own[...].astype(F32) + d_side[...].astype(F32)) + (d_far[...].astype(F32) + d_corner[...].astype(F32))
    res = resid[...]
    scale = rms_scale(res)
    normed = res * scale
    g_norm[...] = jnp.sum(d_hidden * normed, axis=0, keepdims=True)
    d_normed = d_hidden * gain[...]
    out[...] = (grad[...].astype(F32) + scale * (
        d_normed - normed * jnp.mean(d_normed * normed, axis=1, keepdims=True))).astype(BF16)


def second_norm(chunk, info, pieces, resid, grad, gain):
    block, width = pieces[0].shape
    same = pl.BlockSpec((block, width), lambda i, *_: (0, 0))
    return pl.pallas_call(
        second_norm_body,
        grid_spec=pltpu.PrefetchScalarGridSpec(
            num_scalar_prefetch=1,
            grid=(1,),
            in_specs=[same, same, same, same,
                      pl.BlockSpec((block, width), lambda i, info: (chunk, 0)),
                      pl.BlockSpec((block, width), lambda i, info: (4 * chunk + info[2], 0)),
                      resident(gain)],
            out_specs=[same, pl.BlockSpec((1, width), lambda i, *_: (0, 0))],
        ),
        out_shape=[shape((block, width), BF16), shape((1, width), F32)],
        compiler_params=params(),
        cost_estimate=cost(0, 14 * block * width),
        name="second_norm",
    )(info, *pieces, resid, grad, gain)


def place_body(info, own, side, far, left, right, *refs):
    target = refs[-1]
    j = pl.program_id(0) % 4
    for k, source in enumerate((own, side, far)):
        @pl.when(j == k)
        def _():
            target[...] = source[...]

    @pl.when(j == 3)
    def _():
        target[:, :left.shape[1]] = left[...]
        target[:, left.shape[1]:] = right[...]


def place(first, chunks, info, pieces, rows, into, corner=0):
    width = pieces[0].shape[1]
    block = pieces[0].shape[0] // chunks
    kept = [] if into is None else [into]
    at = [0, 0, 0, corner, corner]
    return pl.pallas_call(
        place_body,
        grid_spec=pltpu.PrefetchScalarGridSpec(
            num_scalar_prefetch=1,
            grid=(4 * chunks,),
            in_specs=[pl.BlockSpec((block, p.shape[1]), lambda i, *_, k=k: (k + i // 4, 0)) for p, k in zip(pieces, at)]
            + [pl.BlockSpec(memory_space=pl.ANY)] * len(kept),
            out_specs=pl.BlockSpec((block, width), lambda i, info: (4 * (first + i // 4) + lax.bitwise_xor(i % 4, info[2]), 0)),
        ),
        out_shape=shape((rows, width), BF16),
        input_output_aliases={6: 0} if kept else {},
        compiler_params=params(),
        cost_estimate=cost(0, 2 * nbytes(*pieces)),
        name="place",
    )(info, *pieces, *kept)


def weight_grad_body(left, right, *refs):
    out = refs[-1]
    out[...] = dot_tn(left[...], right[...]).astype(out.dtype)


def weight_grad(left, right, after=(), first=0, wide=None, dtype=F32):
    rows, high = left.shape
    wide = wide or right.shape[1]
    tile = next(t for t in (768, 640, 512, 384, 256, 128) if wide % t == 0)
    return pl.pallas_call(
        weight_grad_body,
        grid=(wide // tile,),
        in_specs=[resident(left), pl.BlockSpec((rows, tile), lambda i: (0, first // tile + i))]
        + [pl.BlockSpec(memory_space=pl.ANY)] * len(after),
        out_specs=pl.BlockSpec((high, tile), lambda i: (0, i)),
        out_shape=shape((high, wide), dtype),
        compiler_params=params(),
        cost_estimate=cost(2 * rows * high * wide, nbytes(left) + 2 * rows * wide + 4 * high * wide),
        name="weight_grad",
    )(left, right, *after)


def conv_backward(slot, info, total, d_gated, c, conved, taps, carry):
    step = pl.program_id(0)
    rows = d_gated.shape[0]
    d_conv = d_gated * c[...].astype(F32)
    g_c = (d_gated * conved[...].astype(F32)).astype(BF16)
    fresh = lax.rem(info[0] + (total - step) * rows, slot) == 0
    after = jnp.where(fresh, 0.0, carry[...])
    row = lax.broadcasted_iota(jnp.int32, d_conv.shape, 0)
    one = jnp.where(row == rows - 1, after[0:1], pltpu.roll(d_conv, rows - 1, 0))
    two = jnp.where(row == rows - 2, after[0:1], jnp.where(row == rows - 1, after[1:2], pltpu.roll(d_conv, rows - 2, 0)))
    carry[...] = d_conv[0:8]
    tap = taps[...].astype(F32)
    return d_conv, one, two, g_c, tap[2:3] * d_conv + tap[1:2] * one + tap[0:1] * two


def own_backward_body(slot, info, grl, p_b, p_c, p_x, conved, h1, gated, next_grl, next_c, w_out, taps, *refs):
    g_in, g_out, g_conv, carry, g_proj = refs[-5:]

    @pl.when(pl.program_id(0) == 0)
    def _():
        carry[...] = (dot_nt(next_grl[...], w_out[...]) * next_c[...].astype(F32))[0:8]
        for total in (g_in, g_out, g_conv):
            total[...] = jnp.zeros_like(total)

    g_out[...] += dot_tn(gated[...], grl[...])
    own = w_out.shape[0]
    d_conv, one, two, g_c, d_mixed = conv_backward(slot, info, pl.num_programs(0), dot_nt(grl[...], w_out[...]), p_c, conved, taps, carry)
    b = p_b[...].astype(F32)
    xx = p_x[...].astype(F32)
    mixed = (b * xx).astype(BF16).astype(F32)
    g_proj[:, :own] = (d_mixed * xx).astype(BF16)
    g_proj[:, own:2 * own] = g_c
    g_proj[:, 2 * own:] = (d_mixed * b).astype(BF16)
    for k, values in enumerate((two, one, d_conv)):
        g_conv[k:k + 1] += jnp.sum(values * mixed, axis=0, keepdims=True)
    g_in[...] += dot_tn(h1[...], g_proj[...])


def own_backward(slot, info, grl, proj, h1, gated, next_grl, next_c, w_out, taps, after=(), tile=512):
    rows, width = grl.shape
    own = w_out.shape[0]
    groups = proj.shape[1] // 4 // own
    steps = rows // tile
    row = lambda n, at=0: pl.BlockSpec((tile, n), lambda i, *_: (steps - 1 - i, at))
    outs = [shape((width, 3 * own), F32), shape((own, width), F32), shape((8, own), F32)]
    ins = [grl, proj, proj, proj, proj, h1, gated, next_grl, next_c, w_out, taps]
    return pl.pallas_call(
        functools.partial(own_backward_body, slot),
        grid_spec=pltpu.PrefetchScalarGridSpec(
            num_scalar_prefetch=1,
            grid=(steps,),
            in_specs=[row(width)] + [row(own, k * groups) for k in range(4)] + [row(width), row(own)]
            + [resident(a) for a in ins[7:]]
            + [pl.BlockSpec(memory_space=pl.ANY)] * len(after),
            out_specs=[pl.BlockSpec(s.shape, lambda i, *_: (0, 0)) for s in outs],
            scratch_shapes=[pltpu.VMEM((8, own), F32), pltpu.VMEM((tile, 3 * own), BF16)],
        ),
        out_shape=outs,
        compiler_params=params(),
        cost_estimate=cost(10 * rows * width * own, nbytes(grl, h1, gated, *outs) + nbytes(proj) // groups),
        name="own_backward",
    )(info, *ins, *after)


def mixer_backward_body(slot, layout, count, total, begun, info, grl, x, p_b, p_c, p_x, conved, next_grl, next_c, gain_one, *refs):
    weights = refs[:count]
    g_in, g_norm, rest, w_all, w_out, taps, sems, carry, held = refs[-9:]
    step = pl.program_id(0)
    chans = w_out.shape[0]

    @pl.when(step == 0)
    def _():
        bring(copies(layout, weights, info[1], w_all, w_out, taps), sems)
        if begun:
            carry[...] = refs[count][...]
        else:
            carry[...] = (dot_nt(next_grl[...], w_out[...]) * next_c[...].astype(F32))[0:8]
        g_norm[...] = jnp.zeros_like(g_norm)

    _, _, _, g_c, d_mixed = conv_backward(slot, info, total, dot_nt(grl[...], w_out[...]), p_c, conved, taps, carry)
    rest[...] = carry[...]
    held[:, :chans] = (d_mixed * p_x[...].astype(F32)).astype(BF16)
    held[:, chans:2 * chans] = g_c
    held[:, 2 * chans:] = (d_mixed * p_b[...].astype(F32)).astype(BF16)
    d_hidden = dot_nt(held[...], w_all[...])
    wide = x[...].astype(F32)
    scale = rms_scale(wide)
    normed = wide * scale
    g_norm[0:1] += jnp.sum(d_hidden * normed, axis=0, keepdims=True)
    d_normed = d_hidden * gain_one[...]
    g_in[...] = grl[...].astype(F32) + scale * (
        d_normed - normed * jnp.mean(d_normed * normed, axis=1, keepdims=True))


def mixer_backward(slot, info, grl, x, proj, next_grl, next_c, gain_one, groups, after=(), part=0, parts=1, kept=(), tile=512):
    rows, width = x.shape
    layout = layout_of(groups)
    chans = sum(size for _, size, _ in layout)
    weights = [a for g in groups for a in group_arrays(g)]
    steps = rows // tile // parts
    total = rows // tile - part * steps
    row = lambda n, at=0: pl.BlockSpec((tile, n), lambda i, *_: (total - 1 - i, at))
    outs = [shape((rows, width), F32), shape((8, width), F32), shape((8, chans), F32)]
    fixed = lambda n: pl.BlockSpec((8, n), lambda i, *_: (0, 0))
    ins = [grl, x, proj, proj, proj, proj, next_grl, next_c, gain_one, *weights, *kept]
    anywhere = pl.BlockSpec(memory_space=pl.ANY)
    return pl.pallas_call(
        functools.partial(mixer_backward_body, slot, layout, len(weights), total, bool(kept)),
        grid_spec=pltpu.PrefetchScalarGridSpec(
            num_scalar_prefetch=1,
            grid=(steps,),
            in_specs=[row(width), row(width)] + [row(chans, k) for k in range(4)]
            + [resident(a) for a in (next_grl, next_c, gain_one)] + [anywhere] * len(weights)
            + ([resident(kept[0]), anywhere] if kept else []) + [anywhere] * len(after),
            out_specs=[row(width), fixed(width), fixed(chans)],
            scratch_shapes=weight_scratch(width, chans, layout)
            + [pltpu.VMEM((8, chans), F32), pltpu.VMEM((tile, 3 * chans), BF16)],
        ),
        out_shape=outs,
        input_output_aliases={len(ins): 0} if kept else {},
        compiler_params=params(),
        cost_estimate=cost(8 * rows * width * chans // parts, nbytes(grl, x, proj, *outs) // parts + nbytes(*weights)),
        name="mixer_backward",
    )(info, *ins, *after)


def swap(value, step):
    count = lax.axis_size("tp")
    return lax.ppermute(value, "tp", [(i, i ^ step) for i in range(count)])


def swap_seq(value, step):
    count = lax.axis_size("seq")
    return lax.ppermute(value, "seq", [(i, i ^ step) for i in range(count)])


def shifted(value, steps):
    count = lax.axis_size("seq")
    return lax.ppermute(value, "seq", [(i, i + steps) for i in range(count) if 0 <= i + steps < count])


def weight_groups(w_in, conv_w, w_out, core, tp):
    own_taps = jnp.concatenate([conv_w, jnp.zeros((13, conv_w.shape[1]), BF16)], axis=0)
    own = ("whole", [w_in, w_out, own_taps])
    width = w_in.shape[1]
    if lax.axis_size("tp") == 4 and w_out.shape[0] == 2 * HALF:
        cut = lambda a, dim: lax.dynamic_slice_in_dim(a, core * HALF, HALF, dim)
        half = pack_half(cut(w_in, 2), cut(conv_w, 1), cut(w_out, 0))
        side, far = swap(half, 1), swap(half, 2)
        low, high = swap(side[:2 * width], 2), swap(far[2 * width:], 1)
        pairs = [("halves", [[side], [swap_seq(side, 1)]]), ("halves", [[far], [swap_seq(far, 1)]])]
        corner = ("halves", [[low, high], [swap_seq(low, 1), swap_seq(high, 1)]])
        return [own, *pairs, corner]
    every = [lax.all_gather(a, "tp") for a in own[1]]
    take = lambda a, j: lax.dynamic_index_in_dim(a, tp ^ j, 0, keepdims=False)
    return [own] + [("whole", [take(a, j) for a in every]) for j in range(1, lax.axis_size("tp"))]


def exchange(blocks):
    return [blocks[0]] + [swap(blocks[j], j) for j in (3, 1, 2)]


def to_sides(own):
    return [swap(own, 1), swap(own, 2)]


def corners(sides):
    half = sides[0][0].shape[1] // 2
    low = [far[:, :half] for _, far in sides]
    high = [side[:, half:] for side, _ in sides]
    join = lambda parts: parts[0] if len(parts) == 1 else jnp.concatenate(parts, axis=0)
    return [swap(join(low), 1), swap(join(high), 2)]


class SeqSum:
    def __init__(self, value):
        seq = lax.axis_index("seq")
        self.core = seq & 1
        line = seq >> 1
        self.keep = (line & 1) ^ (line >> 1)
        self.rows = value.shape[0]
        self.value = value

    def cut(self, array, which, count):
        size = self.rows // count
        return lax.dynamic_slice_in_dim(array, which * size, size, 0)

    def pair(self):
        self.sent = swap_seq(self.cut(self.value, 1 - self.core, 2).astype(BF16), 1)

    def near(self):
        self.value = self.cut(self.value, self.core, 2) + self.sent.astype(F32)
        self.sent = swap_seq(self.cut(self.value, 1 - self.keep, 4).astype(BF16), 2)

    def cross(self):
        self.value = (self.cut(self.value, self.keep, 4) + self.sent.astype(F32)).astype(BF16)
        self.sent = swap_seq(self.value, 6)

    def back(self):
        self.value = (self.value.astype(F32) + self.sent.astype(F32)).astype(BF16)
        self.sent = swap_seq(self.value, 2)

    def share(self):
        first = self.keep == 0
        self.value = jnp.concatenate([jnp.where(first, self.value, self.sent), jnp.where(first, self.sent, self.value)], axis=0)
        self.sent = swap_seq(self.value, 1)

    def result(self):
        first = self.core == 0
        return jnp.concatenate(
            [jnp.where(first, self.value, self.sent), jnp.where(first, self.sent, self.value)], axis=0).astype(F32)

    def state(self):
        return self.value, self.sent

    def put(self, state):
        self.value, self.sent = state


def seq_sum(value):
    return lax.psum(value.astype(BF16), "seq").astype(F32)


def small_sum(value):
    if lax.axis_size("seq") != 8:
        return lax.psum(value, "seq")
    for step in (1, 2, 6):
        value = value + swap_seq(value, step)
    return value


def per_device(inputs, w_in, conv_w, w_out, norm_one, norm_two, w_gate, w_up, w_down, lengths, cotangent):
    rows, width = inputs.shape
    own = w_in.shape[2]
    units = w_gate.shape[1]
    slot = rows * lax.axis_size("seq") // SEQS
    group = lax.axis_size("tp")
    tp = lax.axis_index("tp")
    seq = lax.axis_index("seq")
    core = seq & 1
    info = jnp.stack([seq * rows, core, tp]).astype(jnp.int32)
    chunk = rows // CHUNKS
    block = chunk // group
    split = group == 4

    halo = shifted(inputs[rows - 16:], 1)
    groups = weight_groups(w_in, conv_w, w_out, core, tp)
    gain_one = norm_one.astype(F32)[None, :]
    gain_two = norm_two.astype(F32)[None, :]
    extra = -units % 128
    columns = lambda w: jnp.pad(w, ((0, 0), (0, extra)))
    w_gate, w_up, w_down = columns(w_gate), columns(w_up), jnp.pad(w_down, ((0, extra), (0, 0)))
    padded = units + extra

    scatter = lambda a: lax.psum_scatter(a, "tp", scatter_dimension=0, tiled=True)
    gather = lambda a: lax.all_gather(a.astype(BF16), "tp", axis=0, tiled=True)
    tie = lax.optimization_barrier

    def chunk_layer(k, kept, after=()):
        before = halo if k == 0 else inputs[k * chunk - 16:k * chunk]
        return layer(k, CHUNKS, slot, own, info, lengths, inputs, cotangent, before, gain_one, gain_two, groups,
                     w_gate, w_up, w_down, kept, after, block if split else TILE, split)

    if split and lax.axis_size("seq") == 8:
        kept, blocks0 = chunk_layer(0, [])
        terms0 = exchange(blocks0)
        kept, blocks1 = chunk_layer(1, kept)
        kept, blocks1, terms0 = tie((kept, blocks1, terms0))

        share0, norm0 = second_norm(0, info, terms0, kept[7], kept[4], gain_two)
        terms1 = exchange(blocks1)
        sides0 = to_sides(share0)
        kept, blocks2 = chunk_layer(2, kept, [share0])
        kept, blocks2, sides0, terms1 = tie((kept, blocks2, sides0, terms1))

        proj, gated, h1, h2, grad_low, activ, grads, resid = kept[:8]
        terms2 = exchange(blocks2)
        share1, norm1 = second_norm(1, info, terms1, resid, grad_low, gain_two)
        sides1 = to_sides(share1)
        split_at = 2 * padded * 2 // 3
        g_first = weight_grad(h2, grads, [share1], 0, split_at)
        g_first, terms2, activ, share1, grads = tie((g_first, terms2, activ, share1, grads))

        first = SeqSum(g_first)
        first.pair()
        share2, norm2 = second_norm(2, info, terms2, resid, grad_low, gain_two)
        sides2 = to_sides(share2)
        g_down = weight_grad(activ, grad_low, [share2], dtype=BF16)
        g_down, grads, sides1, state = tie((g_down, grads, sides1, first.state()))

        first.put(state)
        first.near()
        corner01 = corners([sides0, sides1])
        next_c = shifted(proj[:16, width:2 * width], -1)
        g_second = weight_grad(h2, grads, [first.value], split_at, 2 * padded - split_at, BF16)
        g_second, corner01, sides2, next_c, state, forward = tie(
            (g_second, corner01, sides2, next_c, first.state(), kept[8:12]))

        first.put(state)
        first.cross()
        corner2 = corners([sides2])
        grl = place(0, 1, info, [share0, *sides0, *corner01], rows, None)
        next_grl = shifted(grl[:16], -1)
        grl = place(1, 1, info, [share1, *sides1, *corner01], rows, grl, 1)
        grl, next_grl, corner2, forward = tie((grl, next_grl, corner2, forward))

        half = width // 2
        moved = [swap(forward[3][:, :half], 1), swap(forward[3][:, half:], 2)]
        grl = place(2, 1, info, [share2, *sides2, *corner2], rows, grl)
        g_in, g_out, g_conv = own_backward(
            slot, info, grl, proj, h1, gated, next_grl, next_c[:, :own], w_out, groups[0][1][2])
        g_in, g_out, g_conv, moved, state = tie((g_in, g_out, g_conv, moved, first.state()))

        first.put(state)
        add = lambda a, b: (a.astype(F32) + b.astype(F32)).astype(BF16)
        from_side, from_far = moved
        far = jnp.concatenate([add(forward[2][:, :half], from_side), forward[2][:, half:]], axis=1)
        side = jnp.concatenate([forward[1][:, :half], add(forward[1][:, half:], from_far)], axis=1)
        terms = [forward[0], swap(side, 1), swap(far, 2)]
        tail_in = SeqSum(jnp.concatenate([g_in, jnp.pad(g_conv[:3].reshape(1, -1), ((0, 15), (0, 0)))], axis=0))
        tail_in.pair()
        tail_out = SeqSum(g_out)
        tail_out.pair()
        first.back()
        g_down, g_second, state, state2 = tie((g_down, g_second, tail_in.state(), tail_out.state()))

        g_down, g_second = lax.psum((g_down, g_second), "seq")
        tail_in.put(state)
        tail_out.put(state2)
        tail_in.near()
        tail_out.near()
        back = lambda k, kept, after: mixer_backward(
            slot, info, grl, inputs, proj, next_grl, next_c, gain_one, groups, after, k, 2, kept)
        grad_inputs, norm_late, rest = back(0, (), [tail_in.value, tail_out.value])
        grad_inputs, norm_late, rest, terms, norm0, norm1, norm2, state, state2, state3 = tie((
            grad_inputs, norm_late, rest, terms, norm0, norm1, norm2, tail_in.state(), tail_out.state(), first.state()))

        tail_in.put(state)
        tail_out.put(state2)
        first.put(state3)
        final = (resid + sum(t.astype(F32) for t in terms)).astype(BF16)
        sides = to_sides(final)
        tail_in.cross()
        tail_out.cross()
        g_norm_two = norm0 + norm1 + norm2
        g_norm_two = g_norm_two + swap(g_norm_two, 1)
        grad_inputs, norm_early, _ = back(1, (rest, grad_inputs), [tail_in.value, tail_out.value, final])
        grad_inputs, norm_early, sides, state, state2, g_norm_two = tie((
            grad_inputs, norm_early, sides, tail_in.state(), tail_out.state(), g_norm_two))

        tail_in.put(state)
        tail_out.put(state2)
        corner = corners([sides])
        tail_in.back()
        tail_out.back()
        g_norm_two = g_norm_two + swap(g_norm_two, 2)
        corner, g_norm_two, state, state2 = tie((corner, g_norm_two, tail_in.state(), tail_out.state()))

        tail_in.put(state)
        tail_out.put(state2)
        norms = jnp.concatenate([norm_early[:1] + norm_late[:1], g_norm_two], axis=0)
        norms = norms + swap_seq(norms, 1)
        tail_in.share()
        tail_out.share()
        first.share()
        output = place(0, CHUNKS, info, [final, *sides, *corner], rows, None)
        output, norms, state, state2, state3 = tie((output, norms, tail_in.state(), tail_out.state(), first.state()))
        g_down, g_second, _ = tie((g_down, g_second, output))

        tail_in.put(state)
        tail_out.put(state2)
        first.put(state3)
        norms = norms + swap_seq(norms, 2)
        g_out = tail_out.result()
        g_in = tail_in.result()
        g_conv = g_in[width].reshape(3, own)
        norms, g_out, g_in, g_conv = tie((norms, g_out, g_in, g_conv))
        norms = norms + swap_seq(norms, 6)
        g_norm_one, g_norm_two = norms[0], norms[1]
        g_first = first.result()
        g_gu = jnp.concatenate([g_first, g_second.astype(F32)], axis=1)
        g_down = g_down.astype(F32)
    else:
        kept, finals, shares, g_norm_two = [], [], [], 0.0
        cut = lambda a, k: lax.dynamic_slice_in_dim(a, k * chunk + tp * block, block, 0)
        whole = lambda blocks: blocks[0] if not split else jnp.concatenate(
            [lax.dynamic_index_in_dim(jnp.stack(blocks), tp ^ j, 0, keepdims=False) for j in range(4)], axis=0)
        for k in range(CHUNKS):
            kept, blocks = chunk_layer(k, kept)
            terms = kept[8:12] if split else blocks[:1]
            terms = [t[k * block:(k + 1) * block] for t in terms] if split else terms
            d_hidden = scatter(whole(blocks if split else blocks[1:])).astype(F32)
            res = kept[7][k * block:(k + 1) * block] if split else cut(kept[7], k)
            finals.append(gather(res + scatter(whole(terms)).astype(F32)))
            scale = rms_scale(res)
            normed = res * scale
            d_normed = d_hidden * gain_two
            g_norm_two += jnp.sum(d_hidden * normed, axis=0)
            shares.append(gather(cut(kept[4], k).astype(F32) + scale * (
                d_normed - normed * jnp.mean(d_normed * normed, axis=1, keepdims=True))))
        proj, gated, h1, h2, grad_low, activ, grads, resid = kept[:8]
        grl = jnp.concatenate(shares, axis=0)
        output = jnp.concatenate(finals, axis=0)
        g_norm_two = lax.psum(g_norm_two, "tp")
        next_c = shifted(proj[:16, width:2 * width], -1)
        next_grl = shifted(grl[:16], -1)
        g_in, g_out, g_conv = own_backward(
            slot, info, grl, proj, h1, gated, next_grl, next_c[:, :own], w_out, groups[0][1][2])
        grad_inputs, g_norm_one, _ = mixer_backward(slot, info, grl, inputs, proj, next_grl, next_c, gain_one, groups)
        g_norm_one = small_sum(g_norm_one[0])
        g_down = seq_sum(weight_grad(activ, grad_low))
        g_gu = seq_sum(weight_grad(h2, grads))
        g_out = seq_sum(g_out)
        g_in = seq_sum(g_in)
        g_conv = lax.psum(g_conv[:3], "seq")
        g_norm_two = lax.psum(g_norm_two, "seq")
    g_in = g_in[:width]
    return (
        output,
        grad_inputs,
        jnp.stack([g_in[:, i * own:(i + 1) * own] for i in range(3)]),
        g_conv,
        g_out,
        g_norm_one,
        g_norm_two,
        g_gu[:, :units],
        g_gu[:, padded:padded + units],
        g_down[:units],
    )


def solution(mesh):
    tokens = P("seq", None)
    columns = P(None, "tp")
    lines = P("tp", None)
    stacked = P(None, None, "tp")
    return jax.shard_map(
        per_device,
        mesh=mesh,
        in_specs=(tokens, stacked, columns, lines, P(), P(), columns, columns, lines, P(), tokens),
        out_specs=(tokens, tokens, stacked, columns, lines, P(), P(), columns, columns, lines),
        check_vma=False,
    )
```

```python
import functools

import jax
import jax.numpy as jnp
from jax import lax
from jax.experimental import pallas as pl
from jax.experimental.pallas import tpu as pltpu
from jax.sharding import PartitionSpec as P

SEQS = 6
F32 = jnp.float32
BF16 = jnp.bfloat16
VMEM_LIMIT = 56 * 2**20
TILE = 256
CHUNKS = 3


def params():
    return pltpu.CompilerParams(vmem_limit_bytes=VMEM_LIMIT)


def cost(flops, moved):
    return pl.CostEstimate(flops=int(flops), bytes_accessed=int(moved), transcendentals=0)


def nbytes(*arrays):
    return sum(a.size * a.dtype.itemsize for a in arrays)


def shape(dims, dtype):
    return jax.ShapeDtypeStruct(dims, dtype)


def dot(left, right):
    return jnp.dot(left, right, preferred_element_type=F32)


def dot_nt(left, right):
    return lax.dot_general(left, right, (((1,), (1,)), ((), ())), preferred_element_type=F32)


def dot_tn(left, right):
    return lax.dot_general(left, right, (((0,), (0,)), ((), ())), preferred_element_type=F32)


def rms_scale(values):
    return lax.rsqrt(jnp.mean(values * values, axis=1, keepdims=True) + 1e-05)


def resident(array):
    zeros = (0,) * array.ndim
    return pl.BlockSpec(array.shape, lambda i, *_: zeros, pipeline_mode=pl.Buffered(1))


HALF = 128


def pack_half(w_in, conv_w, w_out):
    width = w_in.shape[1]
    out = w_out.reshape(HALF, width // HALF, HALF).transpose(1, 0, 2).reshape(width, HALF)
    taps = jnp.concatenate([conv_w, jnp.zeros((13, HALF), BF16)], axis=0)
    return jnp.concatenate([w_in.reshape(3 * width, HALF), out, taps], axis=0)


def group_arrays(group):
    kind, arrays = group
    return list(arrays) if kind == "whole" else [a for half in arrays for a in half]


def channels_of(group):
    kind, arrays = group
    return arrays[1].shape[0] if kind == "whole" else 2 * HALF


def copies(layout, refs, core, w_all, w_out, taps):
    width = w_all.shape[0]
    chans = w_out.shape[0]
    pairs, at, refs = [], 0, list(refs)
    for kind, size, arrays in layout:
        if kind == "whole":
            w_in, w_o, tap = (refs.pop(0) for _ in range(3))
            for i in range(3):
                pairs.append((w_in.at[i], w_all.at[:, pl.ds(i * chans + at, size)]))
            pairs.append((w_o, w_out.at[pl.ds(at, size), :]))
            pairs.append((tap, taps.at[:, pl.ds(at, size)]))
        else:
            for which, count in enumerate(arrays):
                parts = [refs.pop(0) for _ in range(count)]
                core_of = core if which == 0 else 1 - core
                place = at + core_of * HALF

                def rows(first, length):
                    if len(parts) == 1 or first < 2 * width:
                        return parts[0].at[pl.ds(first, length), :]
                    return parts[1].at[pl.ds(first - 2 * width, length), :]

                for i in range(3):
                    spot = pl.multiple_of(i * chans + place, HALF)
                    pairs.append((rows(i * width, width), w_all.at[:, pl.ds(spot, HALF)]))
                spot = pl.multiple_of(place, HALF)
                for j in range(width // HALF):
                    pairs.append((rows(3 * width + j * HALF, HALF), w_out.at[pl.ds(spot, HALF), pl.ds(j * HALF, HALF)]))
                pairs.append((rows(4 * width, 16), taps.at[:, pl.ds(spot, HALF)]))
        at += size
    return pairs


def layout_of(groups):
    return [(kind, channels_of((kind, arrays)), None if kind == "whole" else [len(h) for h in arrays])
            for kind, arrays in groups]


def copy_count(layout, width):
    per_half = 4 + width // HALF
    return sum(5 if kind == "whole" else 2 * per_half for kind, _, _ in layout)


def bring(pairs, sems):
    handles = [pltpu.make_async_copy(a, b, sems.at[k]) for k, (a, b) in enumerate(pairs)]
    for h in handles:
        h.start()
    for h in handles:
        h.wait()


def weight_scratch(width, chans, layout):
    return [
        pltpu.VMEM((width, 3 * chans), BF16),
        pltpu.VMEM((chans, width), BF16),
        pltpu.VMEM((16, chans), BF16),
        pltpu.SemaphoreType.DMA((copy_count(layout, width),)),
    ]


def layer_body(slot, own, layout, chunk_start, split, counts, info, lens, *refs):
    refs = list(refs)
    x, cot, halo, gain_one, gain_two = (refs.pop(0) for _ in range(5))
    weights = [refs.pop(0) for _ in range(counts[0])]
    w_gate, w_up, w_down = (refs.pop(0) for _ in range(3))
    del refs[:counts[1]]
    proj, gated, h1, h2, grad, activ, grads, resid = (refs.pop(0) for _ in range(8))
    forward = [refs.pop(0) for _ in range(4 if split else 1)]
    backward = [refs.pop(0) for _ in range(4 if split else 1)]
    w_all, w_out, taps, sems, w_gu, w_dn, more, carry = refs
    step = pl.program_id(0)
    rows, width = x.shape
    chans = w_out.shape[0]
    units = w_dn.shape[0]
    place = info[0] + chunk_start + step * rows

    def late():
        pairs = [(w_gate, w_gu.at[:, pl.ds(0, units)]), (w_up, w_gu.at[:, pl.ds(units, units)]), (w_down, w_dn)]
        return [pltpu.make_async_copy(a, b, more.at[k]) for k, (a, b) in enumerate(pairs)]

    def hidden(wide):
        return ((wide * rms_scale(wide)) * gain_one[...]).astype(BF16)

    @pl.when(step == 0)
    def _():
        early = [pltpu.make_async_copy(a, b, sems.at[k])
                 for k, (a, b) in enumerate(copies(layout, weights, info[1], w_all, w_out, taps))]
        for h in early:
            h.start()
        for h in late():
            h.start()
        for h in early:
            h.wait()
        for h in late():
            h.wait()
        before = dot(hidden(halo[...].astype(F32)), w_all[...])
        mixed = (before[:, :chans] * before[:, 2 * chans:]).astype(BF16).astype(F32)
        carry[...] = mixed[8:16]

    wide = x[...].astype(F32)
    low = hidden(wide)
    h1[...] = low
    every = dot(low, w_all[...])
    b, c, xx = (every[:, i * chans:(i + 1) * chans] for i in range(3))
    mixed = (b * xx).astype(BF16).astype(F32)
    before = jnp.where(lax.rem(place, slot) == 0, 0.0, carry[...])
    row = lax.broadcasted_iota(jnp.int32, mixed.shape, 0)
    one = jnp.where(row == 0, before[7:8], pltpu.roll(mixed, 1, 0))
    two = jnp.where(row == 0, before[6:7], jnp.where(row == 1, before[7:8], pltpu.roll(mixed, 2, 0)))
    carry[...] = mixed[rows - 8:]
    tap = taps[...].astype(F32)
    conved = tap[2:3] * mixed + tap[1:2] * one + tap[0:1] * two
    gate = (c * conved).astype(BF16)
    for i, part in enumerate((b, c, xx, conved)):
        proj[:, i * chans:(i + 1) * chans] = part.astype(BF16)
    gated[...] = gate[:, :own]
    res = wide + dot(gate, w_out[...])
    post = ((res * rms_scale(res)) * gain_two[...]).astype(BF16)
    h2[...] = post
    limit = lens[lax.div(place, slot)] - lax.rem(place, slot)
    line = lax.broadcasted_iota(jnp.int32, (rows, width), 0)
    low_grad = jnp.where(line < limit, cot[...].astype(F32), 0.0).astype(BF16)
    grad[...] = low_grad

    both = dot(post, w_gu[...])
    d_activ = dot_nt(low_grad, w_dn[...])
    pre = both[:, :units]
    up = both[:, units:]
    sig = 1.0 / (1.0 + jnp.exp(-pre))
    silu = pre * sig
    act = (silu * up).astype(BF16)
    g_gate = (d_activ * up * sig * (1.0 + pre * (1.0 - sig))).astype(BF16)
    g_up = (d_activ * silu).astype(BF16)
    activ[...] = act
    grads[:, :units] = g_gate
    grads[:, units:] = g_up
    back = dot_nt(grads[...], w_gu[...]).astype(BF16)
    out = dot(act, w_dn[...]).astype(BF16)
    if not split:
        forward[0][...] = out
        resid[...] = res
        backward[0][...] = back
        return
    far = lax.bitwise_xor(step, info[2])
    for j in range(4):
        @pl.when(far == j)
        def _():
            backward[j][...] = back
            forward[j][...] = out
            if j == 0:
                resid[...] = res


def layer(chunk, chunks, slot, own, info, lens, x, cot, halo, gain_one, gain_two, groups, w_gate, w_up, w_down, kept, after, tile, split):
    rows, width = x.shape
    layout = layout_of(groups)
    chans = sum(size for _, size, _ in layout)
    units = w_down.shape[0]
    weights = [a for g in groups for a in group_arrays(g)]
    steps = rows // chunks // tile
    row = lambda n: pl.BlockSpec((tile, n), lambda i, *_: (chunk * steps + i, 0))
    once = lambda n, at: pl.BlockSpec((tile, n), lambda i, *_: (at, 0))
    anywhere = pl.BlockSpec(memory_space=pl.ANY)
    outs = [shape((rows, 4 * chans), BF16), shape((rows, own), BF16), shape((rows, width), BF16),
            shape((rows, width), BF16), shape((rows, width), BF16), shape((rows, units), BF16), shape((rows, 2 * units), BF16)]
    specs = [row(s.shape[1]) for s in outs]
    part = pl.BlockSpec((tile, width), lambda i, *_: (i, 0))
    sums = shape((rows // chunks, width), BF16)
    if split:
        outs += [shape((chunks * tile, width), F32)] + [shape((chunks * tile, width), BF16)] * 4
        outs += [shape((tile, width), BF16)] * 4
        specs += [once(width, chunk)] * 5 + [once(width, 0)] * 4
    else:
        outs += [shape((rows, width), F32), sums, sums]
        specs += [row(width), part, part]
    ins = [x, cot, halo, gain_one, gain_two, *weights, w_gate, w_up, w_down, *kept, *after]
    result = pl.pallas_call(
        functools.partial(layer_body, slot, own, layout, chunk * steps * tile, split, (len(weights), len(kept) + len(after))),
        grid_spec=pltpu.PrefetchScalarGridSpec(
            num_scalar_prefetch=2,
            grid=(steps,),
            in_specs=[row(width), row(width)] + [resident(a) for a in (halo, gain_one, gain_two)]
            + [anywhere] * (len(weights) + 3 + len(kept) + len(after)),
            out_specs=specs,
            scratch_shapes=weight_scratch(width, chans, layout) + [
                pltpu.VMEM((width, 2 * units), BF16), pltpu.VMEM((units, width), BF16),
                pltpu.SemaphoreType.DMA((3,)), pltpu.VMEM((8, chans), F32)],
        ),
        out_shape=outs,
        input_output_aliases={2 + len(ins) - len(kept) - len(after) + k: k for k in range(len(kept))},
        compiler_params=params(),
        cost_estimate=cost(steps * tile * width * (8 * chans + 12 * units),
                           nbytes(x, cot, *outs[:7]) // chunks + nbytes(*weights, w_gate, w_up, w_down)),
        name="layer",
    )(info, lens, *ins)
    shared = 12 if split else 8
    return result[:shared], result[shared:]


def second_norm_body(info, d_own, d_side, d_far, d_corner, resid, grad, gain, out, g_norm):
    d_hidden = (d_own[...].astype(F32) + d_side[...].astype(F32)) + (d_far[...].astype(F32) + d_corner[...].astype(F32))
    res = resid[...]
    scale = rms_scale(res)
    normed = res * scale
    g_norm[...] = jnp.sum(d_hidden * normed, axis=0, keepdims=True)
    d_normed = d_hidden * gain[...]
    out[...] = (grad[...].astype(F32) + scale * (
        d_normed - normed * jnp.mean(d_normed * normed, axis=1, keepdims=True))).astype(BF16)


def second_norm(chunk, info, pieces, resid, grad, gain):
    block, width = pieces[0].shape
    same = pl.BlockSpec((block, width), lambda i, *_: (0, 0))
    return pl.pallas_call(
        second_norm_body,
        grid_spec=pltpu.PrefetchScalarGridSpec(
            num_scalar_prefetch=1,
            grid=(1,),
            in_specs=[same, same, same, same,
                      pl.BlockSpec((block, width), lambda i, info: (chunk, 0)),
                      pl.BlockSpec((block, width), lambda i, info: (4 * chunk + info[2], 0)),
                      resident(gain)],
            out_specs=[same, pl.BlockSpec((1, width), lambda i, *_: (0, 0))],
        ),
        out_shape=[shape((block, width), BF16), shape((1, width), F32)],
        compiler_params=params(),
        cost_estimate=cost(0, 14 * block * width),
        name="second_norm",
    )(info, *pieces, resid, grad, gain)


def place_body(info, own, side, far, left, right, *refs):
    target = refs[-1]
    j = pl.program_id(0) % 4
    for k, source in enumerate((own, side, far)):
        @pl.when(j == k)
        def _():
            target[...] = source[...]

    @pl.when(j == 3)
    def _():
        target[:, :left.shape[1]] = left[...]
        target[:, left.shape[1]:] = right[...]


def place(first, chunks, info, pieces, rows, into, corner=0):
    width = pieces[0].shape[1]
    block = pieces[0].shape[0] // chunks
    kept = [] if into is None else [into]
    at = [0, 0, 0, corner, corner]
    return pl.pallas_call(
        place_body,
        grid_spec=pltpu.PrefetchScalarGridSpec(
            num_scalar_prefetch=1,
            grid=(4 * chunks,),
            in_specs=[pl.BlockSpec((block, p.shape[1]), lambda i, *_, k=k: (k + i // 4, 0)) for p, k in zip(pieces, at)]
            + [pl.BlockSpec(memory_space=pl.ANY)] * len(kept),
            out_specs=pl.BlockSpec((block, width), lambda i, info: (4 * (first + i // 4) + lax.bitwise_xor(i % 4, info[2]), 0)),
        ),
        out_shape=shape((rows, width), BF16),
        input_output_aliases={6: 0} if kept else {},
        compiler_params=params(),
        cost_estimate=cost(0, 2 * nbytes(*pieces)),
        name="place",
    )(info, *pieces, *kept)


def weight_grad_body(left, right, *refs):
    out = refs[-1]
    out[...] = dot_tn(left[...], right[...]).astype(out.dtype)


def weight_grad(left, right, after=(), first=0, wide=None, dtype=F32):
    rows, high = left.shape
    wide = wide or right.shape[1]
    tile = next(t for t in (768, 640, 512, 384, 256, 128) if wide % t == 0)
    return pl.pallas_call(
        weight_grad_body,
        grid=(wide // tile,),
        in_specs=[resident(left), pl.BlockSpec((rows, tile), lambda i: (0, first // tile + i))]
        + [pl.BlockSpec(memory_space=pl.ANY)] * len(after),
        out_specs=pl.BlockSpec((high, tile), lambda i: (0, i)),
        out_shape=shape((high, wide), dtype),
        compiler_params=params(),
        cost_estimate=cost(2 * rows * high * wide, nbytes(left) + 2 * rows * wide + 4 * high * wide),
        name="weight_grad",
    )(left, right, *after)


def conv_backward(slot, info, total, d_gated, c, conved, taps, carry):
    step = pl.program_id(0)
    rows = d_gated.shape[0]
    d_conv = d_gated * c[...].astype(F32)
    g_c = (d_gated * conved[...].astype(F32)).astype(BF16)
    fresh = lax.rem(info[0] + (total - step) * rows, slot) == 0
    after = jnp.where(fresh, 0.0, carry[...])
    row = lax.broadcasted_iota(jnp.int32, d_conv.shape, 0)
    one = jnp.where(row == rows - 1, after[0:1], pltpu.roll(d_conv, rows - 1, 0))
    two = jnp.where(row == rows - 2, after[0:1], jnp.where(row == rows - 1, after[1:2], pltpu.roll(d_conv, rows - 2, 0)))
    carry[...] = d_conv[0:8]
    tap = taps[...].astype(F32)
    return d_conv, one, two, g_c, tap[2:3] * d_conv + tap[1:2] * one + tap[0:1] * two


def own_backward_body(slot, info, grl, p_b, p_c, p_x, conved, h1, gated, next_grl, next_c, w_out, taps, *refs):
    g_in, g_out, g_conv, carry, g_proj = refs[-5:]

    @pl.when(pl.program_id(0) == 0)
    def _():
        carry[...] = (dot_nt(next_grl[...], w_out[...]) * next_c[...].astype(F32))[0:8]
        for total in (g_in, g_out, g_conv):
            total[...] = jnp.zeros_like(total)

    g_out[...] += dot_tn(gated[...], grl[...])
    own = w_out.shape[0]
    d_conv, one, two, g_c, d_mixed = conv_backward(slot, info, pl.num_programs(0), dot_nt(grl[...], w_out[...]), p_c, conved, taps, carry)
    b = p_b[...].astype(F32)
    xx = p_x[...].astype(F32)
    mixed = (b * xx).astype(BF16).astype(F32)
    g_proj[:, :own] = (d_mixed * xx).astype(BF16)
    g_proj[:, own:2 * own] = g_c
    g_proj[:, 2 * own:] = (d_mixed * b).astype(BF16)
    for k, values in enumerate((two, one, d_conv)):
        g_conv[k:k + 1] += jnp.sum(values * mixed, axis=0, keepdims=True)
    g_in[...] += dot_tn(h1[...], g_proj[...])


def own_backward(slot, info, grl, proj, h1, gated, next_grl, next_c, w_out, taps, after=(), tile=512):
    rows, width = grl.shape
    own = w_out.shape[0]
    groups = proj.shape[1] // 4 // own
    steps = rows // tile
    row = lambda n, at=0: pl.BlockSpec((tile, n), lambda i, *_: (steps - 1 - i, at))
    outs = [shape((width, 3 * own), F32), shape((own, width), F32), shape((8, own), F32)]
    ins = [grl, proj, proj, proj, proj, h1, gated, next_grl, next_c, w_out, taps]
    return pl.pallas_call(
        functools.partial(own_backward_body, slot),
        grid_spec=pltpu.PrefetchScalarGridSpec(
            num_scalar_prefetch=1,
            grid=(steps,),
            in_specs=[row(width)] + [row(own, k * groups) for k in range(4)] + [row(width), row(own)]
            + [resident(a) for a in ins[7:]]
            + [pl.BlockSpec(memory_space=pl.ANY)] * len(after),
            out_specs=[pl.BlockSpec(s.shape, lambda i, *_: (0, 0)) for s in outs],
            scratch_shapes=[pltpu.VMEM((8, own), F32), pltpu.VMEM((tile, 3 * own), BF16)],
        ),
        out_shape=outs,
        compiler_params=params(),
        cost_estimate=cost(10 * rows * width * own, nbytes(grl, h1, gated, *outs) + nbytes(proj) // groups),
        name="own_backward",
    )(info, *ins, *after)


def mixer_backward_body(slot, layout, count, total, begun, info, grl, x, p_b, p_c, p_x, conved, next_grl, next_c, gain_one, *refs):
    weights = refs[:count]
    g_in, g_norm, rest, w_all, w_out, taps, sems, carry, held = refs[-9:]
    step = pl.program_id(0)
    chans = w_out.shape[0]

    @pl.when(step == 0)
    def _():
        bring(copies(layout, weights, info[1], w_all, w_out, taps), sems)
        if begun:
            carry[...] = refs[count][...]
        else:
            carry[...] = (dot_nt(next_grl[...], w_out[...]) * next_c[...].astype(F32))[0:8]
        g_norm[...] = jnp.zeros_like(g_norm)

    _, _, _, g_c, d_mixed = conv_backward(slot, info, total, dot_nt(grl[...], w_out[...]), p_c, conved, taps, carry)
    rest[...] = carry[...]
    held[:, :chans] = (d_mixed * p_x[...].astype(F32)).astype(BF16)
    held[:, chans:2 * chans] = g_c
    held[:, 2 * chans:] = (d_mixed * p_b[...].astype(F32)).astype(BF16)
    d_hidden = dot_nt(held[...], w_all[...])
    wide = x[...].astype(F32)
    scale = rms_scale(wide)
    normed = wide * scale
    g_norm[0:1] += jnp.sum(d_hidden * normed, axis=0, keepdims=True)
    d_normed = d_hidden * gain_one[...]
    g_in[...] = grl[...].astype(F32) + scale * (
        d_normed - normed * jnp.mean(d_normed * normed, axis=1, keepdims=True))


def mixer_backward(slot, info, grl, x, proj, next_grl, next_c, gain_one, groups, after=(), part=0, parts=1, kept=(), tile=512):
    rows, width = x.shape
    layout = layout_of(groups)
    chans = sum(size for _, size, _ in layout)
    weights = [a for g in groups for a in group_arrays(g)]
    steps = rows // tile // parts
    total = rows // tile - part * steps
    row = lambda n, at=0: pl.BlockSpec((tile, n), lambda i, *_: (total - 1 - i, at))
    outs = [shape((rows, width), F32), shape((8, width), F32), shape((8, chans), F32)]
    fixed = lambda n: pl.BlockSpec((8, n), lambda i, *_: (0, 0))
    ins = [grl, x, proj, proj, proj, proj, next_grl, next_c, gain_one, *weights, *kept]
    anywhere = pl.BlockSpec(memory_space=pl.ANY)
    return pl.pallas_call(
        functools.partial(mixer_backward_body, slot, layout, len(weights), total, bool(kept)),
        grid_spec=pltpu.PrefetchScalarGridSpec(
            num_scalar_prefetch=1,
            grid=(steps,),
            in_specs=[row(width), row(width)] + [row(chans, k) for k in range(4)]
            + [resident(a) for a in (next_grl, next_c, gain_one)] + [anywhere] * len(weights)
            + ([resident(kept[0]), anywhere] if kept else []) + [anywhere] * len(after),
            out_specs=[row(width), fixed(width), fixed(chans)],
            scratch_shapes=weight_scratch(width, chans, layout)
            + [pltpu.VMEM((8, chans), F32), pltpu.VMEM((tile, 3 * chans), BF16)],
        ),
        out_shape=outs,
        input_output_aliases={len(ins): 0} if kept else {},
        compiler_params=params(),
        cost_estimate=cost(8 * rows * width * chans // parts, nbytes(grl, x, proj, *outs) // parts + nbytes(*weights)),
        name="mixer_backward",
    )(info, *ins, *after)


def swap(value, step):
    count = lax.axis_size("tp")
    return lax.ppermute(value, "tp", [(i, i ^ step) for i in range(count)])


def swap_seq(value, step):
    count = lax.axis_size("seq")
    return lax.ppermute(value, "seq", [(i, i ^ step) for i in range(count)])


def shifted(value, steps):
    count = lax.axis_size("seq")
    return lax.ppermute(value, "seq", [(i, i + steps) for i in range(count) if 0 <= i + steps < count])


def weight_groups(w_in, conv_w, w_out, core, tp):
    own_taps = jnp.concatenate([conv_w, jnp.zeros((13, conv_w.shape[1]), BF16)], axis=0)
    own = ("whole", [w_in, w_out, own_taps])
    width = w_in.shape[1]
    if lax.axis_size("tp") == 4 and w_out.shape[0] == 2 * HALF:
        cut = lambda a, dim: lax.dynamic_slice_in_dim(a, core * HALF, HALF, dim)
        half = pack_half(cut(w_in, 2), cut(conv_w, 1), cut(w_out, 0))
        side, far = swap(half, 1), swap(half, 2)
        low, high = swap(side[:2 * width], 2), swap(far[2 * width:], 1)
        pairs = [("halves", [[side], [swap_seq(side, 1)]]), ("halves", [[far], [swap_seq(far, 1)]])]
        corner = ("halves", [[low, high], [swap_seq(low, 1), swap_seq(high, 1)]])
        return [own, *pairs, corner]
    every = [lax.all_gather(a, "tp") for a in own[1]]
    take = lambda a, j: lax.dynamic_index_in_dim(a, tp ^ j, 0, keepdims=False)
    return [own] + [("whole", [take(a, j) for a in every]) for j in range(1, lax.axis_size("tp"))]


def exchange(blocks):
    return [blocks[0]] + [swap(blocks[j], j) for j in (3, 1, 2)]


def to_sides(own):
    return [swap(own, 1), swap(own, 2)]


def corners(sides):
    half = sides[0][0].shape[1] // 2
    low = [far[:, :half] for _, far in sides]
    high = [side[:, half:] for side, _ in sides]
    join = lambda parts: parts[0] if len(parts) == 1 else jnp.concatenate(parts, axis=0)
    return [swap(join(low), 1), swap(join(high), 2)]


class SeqSum:
    def __init__(self, value):
        seq = lax.axis_index("seq")
        self.core = seq & 1
        line = seq >> 1
        self.keep = (line & 1) ^ (line >> 1)
        self.rows = value.shape[0]
        self.value = value

    def cut(self, array, which, count):
        size = self.rows // count
        return lax.dynamic_slice_in_dim(array, which * size, size, 0)

    def pair(self):
        self.sent = swap_seq(self.cut(self.value, 1 - self.core, 2).astype(BF16), 1)

    def near(self):
        self.value = self.cut(self.value, self.core, 2) + self.sent.astype(F32)
        self.sent = swap_seq(self.cut(self.value, 1 - self.keep, 4).astype(BF16), 2)

    def cross(self):
        self.value = (self.cut(self.value, self.keep, 4) + self.sent.astype(F32)).astype(BF16)
        self.sent = swap_seq(self.value, 6)

    def back(self):
        self.value = (self.value.astype(F32) + self.sent.astype(F32)).astype(BF16)
        self.sent = swap_seq(self.value, 2)

    def share(self):
        first = self.keep == 0
        self.value = jnp.concatenate([jnp.where(first, self.value, self.sent), jnp.where(first, self.sent, self.value)], axis=0)
        self.sent = swap_seq(self.value, 1)

    def result(self):
        first = self.core == 0
        return jnp.concatenate(
            [jnp.where(first, self.value, self.sent), jnp.where(first, self.sent, self.value)], axis=0).astype(F32)

    def state(self):
        return self.value, self.sent

    def put(self, state):
        self.value, self.sent = state


def seq_sum(value):
    return lax.psum(value.astype(BF16), "seq").astype(F32)


def small_sum(value):
    if lax.axis_size("seq") != 8:
        return lax.psum(value, "seq")
    for step in (1, 2, 6):
        value = value + swap_seq(value, step)
    return value


def per_device(inputs, w_in, conv_w, w_out, norm_one, norm_two, w_gate, w_up, w_down, lengths, cotangent):
    rows, width = inputs.shape
    own = w_in.shape[2]
    units = w_gate.shape[1]
    slot = rows * lax.axis_size("seq") // SEQS
    group = lax.axis_size("tp")
    tp = lax.axis_index("tp")
    seq = lax.axis_index("seq")
    core = seq & 1
    info = jnp.stack([seq * rows, core, tp]).astype(jnp.int32)
    chunk = rows // CHUNKS
    block = chunk // group
    split = group == 4

    halo = shifted(inputs[rows - 16:], 1)
    groups = weight_groups(w_in, conv_w, w_out, core, tp)
    gain_one = norm_one.astype(F32)[None, :]
    gain_two = norm_two.astype(F32)[None, :]
    extra = -units % 128
    columns = lambda w: jnp.pad(w, ((0, 0), (0, extra)))
    w_gate, w_up, w_down = columns(w_gate), columns(w_up), jnp.pad(w_down, ((0, extra), (0, 0)))
    padded = units + extra

    scatter = lambda a: lax.psum_scatter(a, "tp", scatter_dimension=0, tiled=True)
    gather = lambda a: lax.all_gather(a.astype(BF16), "tp", axis=0, tiled=True)
    tie = lax.optimization_barrier

    def chunk_layer(k, kept, after=()):
        before = halo if k == 0 else inputs[k * chunk - 16:k * chunk]
        return layer(k, CHUNKS, slot, own, info, lengths, inputs, cotangent, before, gain_one, gain_two, groups,
                     w_gate, w_up, w_down, kept, after, block if split else TILE, split)

    if split and lax.axis_size("seq") == 8:
        kept, blocks0 = chunk_layer(0, [])
        terms0 = exchange(blocks0)
        kept, blocks1 = chunk_layer(1, kept)
        kept, blocks1, terms0 = tie((kept, blocks1, terms0))

        share0, norm0 = second_norm(0, info, terms0, kept[7], kept[4], gain_two)
        terms1 = exchange(blocks1)
        sides0 = to_sides(share0)
        kept, blocks2 = chunk_layer(2, kept, [share0])
        kept, blocks2, sides0, terms1 = tie((kept, blocks2, sides0, terms1))

        proj, gated, h1, h2, grad_low, activ, grads, resid = kept[:8]
        terms2 = exchange(blocks2)
        share1, norm1 = second_norm(1, info, terms1, resid, grad_low, gain_two)
        sides1 = to_sides(share1)
        g_first = weight_grad(h2, grads, [share1])
        g_first, terms2, activ, share1, grads = tie((g_first, terms2, activ, share1, grads))

        first = SeqSum(g_first)
        first.pair()
        share2, norm2 = second_norm(2, info, terms2, resid, grad_low, gain_two)
        sides2 = to_sides(share2)
        g_down = weight_grad(activ, grad_low, [share2], dtype=BF16)
        g_down, grads, sides1, state = tie((g_down, grads, sides1, first.state()))

        first.put(state)
        first.near()
        corner01 = corners([sides0, sides1])
        next_c = shifted(proj[:16, width:2 * width], -1)
        corner01, sides2, next_c, state, forward = tie((corner01, sides2, next_c, first.state(), kept[8:12]))

        first.put(state)
        first.cross()
        corner2 = corners([sides2])
        grl = place(0, 1, info, [share0, *sides0, *corner01], rows, None)
        next_grl = shifted(grl[:16], -1)
        grl = place(1, 1, info, [share1, *sides1, *corner01], rows, grl, 1)
        grl, next_grl, corner2, forward = tie((grl, next_grl, corner2, forward))

        half = width // 2
        moved = [swap(forward[3][:, :half], 1), swap(forward[3][:, half:], 2)]
        grl = place(2, 1, info, [share2, *sides2, *corner2], rows, grl)
        g_in, g_out, g_conv = own_backward(
            slot, info, grl, proj, h1, gated, next_grl, next_c[:, :own], w_out, groups[0][1][2])
        g_in, g_out, g_conv, moved, state = tie((g_in, g_out, g_conv, moved, first.state()))

        first.put(state)
        add = lambda a, b: (a.astype(F32) + b.astype(F32)).astype(BF16)
        from_side, from_far = moved
        far = jnp.concatenate([add(forward[2][:, :half], from_side), forward[2][:, half:]], axis=1)
        side = jnp.concatenate([forward[1][:, :half], add(forward[1][:, half:], from_far)], axis=1)
        terms = [forward[0], swap(side, 1), swap(far, 2)]
        tail_in = SeqSum(jnp.concatenate([g_in, jnp.pad(g_conv[:3].reshape(1, -1), ((0, 15), (0, 0)))], axis=0))
        tail_in.pair()
        tail_out = SeqSum(g_out)
        tail_out.pair()
        first.back()
        g_down, state, state2 = tie((g_down, tail_in.state(), tail_out.state()))

        g_down = lax.psum(g_down, "seq")
        tail_in.put(state)
        tail_out.put(state2)
        tail_in.near()
        tail_out.near()
        back = lambda k, kept, after: mixer_backward(
            slot, info, grl, inputs, proj, next_grl, next_c, gain_one, groups, after, k, 2, kept)
        grad_inputs, norm_late, rest = back(0, (), [tail_in.value, tail_out.value])
        grad_inputs, norm_late, rest, terms, norm0, norm1, norm2, state, state2, state3 = tie((
            grad_inputs, norm_late, rest, terms, norm0, norm1, norm2, tail_in.state(), tail_out.state(), first.state()))

        tail_in.put(state)
        tail_out.put(state2)
        first.put(state3)
        final = (resid + sum(t.astype(F32) for t in terms)).astype(BF16)
        sides = to_sides(final)
        tail_in.cross()
        tail_out.cross()
        g_norm_two = norm0 + norm1 + norm2
        g_norm_two = g_norm_two + swap(g_norm_two, 1)
        grad_inputs, norm_early, _ = back(1, (rest, grad_inputs), [tail_in.value, tail_out.value, final])
        grad_inputs, norm_early, sides, state, state2, g_norm_two, g_down = tie((
            grad_inputs, norm_early, sides, tail_in.state(), tail_out.state(), g_norm_two, g_down))

        tail_in.put(state)
        tail_out.put(state2)
        corner = corners([sides])
        tail_in.back()
        tail_out.back()
        g_norm_two = g_norm_two + swap(g_norm_two, 2)
        corner, g_norm_two, state, state2 = tie((corner, g_norm_two, tail_in.state(), tail_out.state()))

        tail_in.put(state)
        tail_out.put(state2)
        norms = jnp.concatenate([norm_early[:1] + norm_late[:1], g_norm_two], axis=0)
        norms = norms + swap_seq(norms, 1)
        tail_in.share()
        tail_out.share()
        first.share()
        output = place(0, CHUNKS, info, [final, *sides, *corner], rows, None)
        output, norms, state, state2, state3 = tie((output, norms, tail_in.state(), tail_out.state(), first.state()))
        g_down, _ = tie((g_down, output))

        tail_in.put(state)
        tail_out.put(state2)
        first.put(state3)
        norms = norms + swap_seq(norms, 2)
        g_out = tail_out.result()
        g_in = tail_in.result()
        g_conv = g_in[width].reshape(3, own)
        norms, g_out, g_in, g_conv = tie((norms, g_out, g_in, g_conv))
        norms = norms + swap_seq(norms, 6)
        g_norm_one, g_norm_two = norms[0], norms[1]
        g_first = first.result()
        g_gu = g_first
        g_down = g_down.astype(F32)
    else:
        kept, finals, shares, g_norm_two = [], [], [], 0.0
        cut = lambda a, k: lax.dynamic_slice_in_dim(a, k * chunk + tp * block, block, 0)
        whole = lambda blocks: blocks[0] if not split else jnp.concatenate(
            [lax.dynamic_index_in_dim(jnp.stack(blocks), tp ^ j, 0, keepdims=False) for j in range(4)], axis=0)
        for k in range(CHUNKS):
            kept, blocks = chunk_layer(k, kept)
            terms = kept[8:12] if split else blocks[:1]
            terms = [t[k * block:(k + 1) * block] for t in terms] if split else terms
            d_hidden = scatter(whole(blocks if split else blocks[1:])).astype(F32)
            res = kept[7][k * block:(k + 1) * block] if split else cut(kept[7], k)
            finals.append(gather(res + scatter(whole(terms)).astype(F32)))
            scale = rms_scale(res)
            normed = res * scale
            d_normed = d_hidden * gain_two
            g_norm_two += jnp.sum(d_hidden * normed, axis=0)
            shares.append(gather(cut(kept[4], k).astype(F32) + scale * (
                d_normed - normed * jnp.mean(d_normed * normed, axis=1, keepdims=True))))
        proj, gated, h1, h2, grad_low, activ, grads, resid = kept[:8]
        grl = jnp.concatenate(shares, axis=0)
        output = jnp.concatenate(finals, axis=0)
        g_norm_two = lax.psum(g_norm_two, "tp")
        next_c = shifted(proj[:16, width:2 * width], -1)
        next_grl = shifted(grl[:16], -1)
        g_in, g_out, g_conv = own_backward(
            slot, info, grl, proj, h1, gated, next_grl, next_c[:, :own], w_out, groups[0][1][2])
        grad_inputs, g_norm_one, _ = mixer_backward(slot, info, grl, inputs, proj, next_grl, next_c, gain_one, groups)
        g_norm_one = small_sum(g_norm_one[0])
        g_down = seq_sum(weight_grad(activ, grad_low))
        g_gu = seq_sum(weight_grad(h2, grads))
        g_out = seq_sum(g_out)
        g_in = seq_sum(g_in)
        g_conv = lax.psum(g_conv[:3], "seq")
        g_norm_two = lax.psum(g_norm_two, "seq")
    g_in = g_in[:width]
    return (
        output,
        grad_inputs,
        jnp.stack([g_in[:, i * own:(i + 1) * own] for i in range(3)]),
        g_conv,
        g_out,
        g_norm_one,
        g_norm_two,
        g_gu[:, :units],
        g_gu[:, padded:padded + units],
        g_down[:units],
    )


def solution(mesh):
    tokens = P("seq", None)
    columns = P(None, "tp")
    lines = P("tp", None)
    stacked = P(None, None, "tp")
    return jax.shard_map(
        per_device,
        mesh=mesh,
        in_specs=(tokens, stacked, columns, lines, P(), P(), columns, columns, lines, P(), tokens),
        out_specs=(tokens, tokens, stacked, columns, lines, P(), P(), columns, columns, lines),
        check_vma=False,
    )
```
